128 devices in a mesh: seq: 32 (over y, z, core), chan: 4 (over x).
Axes of the slice: x: 4, y: 4, z: 4, core: 2. Of those that a mesh axis runs over, the one named last changes fastest.
Arguments:
- features: bfloat16 [4096, 3, 4096], P('seq', None, 'chan'), may hold values from -6 to 6
- short_taps: float32 [3, 3, 4096], P(None, None, 'chan'), may hold values from -4 to 4
- skip_gain: float32 [4096], P('chan'), may hold values from 0.5 to 1.5
- long_filter: float32 [4096, 4096], P('seq', 'chan'), may hold values from -0.09375 to 0.09375
- out_weight: bfloat16 [4096, 8192], P('chan'), may hold values from -0.125 to 0.125
Outputs:
- layer_out: bfloat16 [4096, 8192], P('seq', 'chan')
The draws below stay inside these ranges and needn't reach their ends.
All inputs are finite; a program needn't handle non-finite values.
Results may differ from the reference program's by a relative error of at most 0.02.
Values may be sent and summed in bfloat16 or wider, within the bound.
No kernel may reach another device: no remote copies, remote signals or barrier semaphores. Data moves between devices by JAX's collectives and lax.ppermute only.
A program may use at most 128 MiB of HBM per device.

```python
import jax
import jax.numpy as jnp
from jax import lax

D = 8192
C = 4096
TOK_DEV = 128
SEQ_LEN = 4096
N_SEQ = 32
N_CHAN = 4


def strengthened(values, own_key, source, target, shards_of, factor):
    owner, partner = [(jnp.arange(values.shape[position]) // (values.shape[position] // shards_of)).reshape([-1 if axis == position else 1 for axis in range(values.ndim)]) for position in (source, target)]
    chosen = jax.random.permutation(own_key, shards_of)[partner]
    strong = (owner == chosen) | (owner == (partner + shards_of // 2) % shards_of)
    return jnp.where(strong, factor * values, values)


def level_of(stream_key, dims, pieces, low, high):
    gain = 1.0
    for position, blocks in pieces:
        draws = jax.random.uniform(jax.random.fold_in(jax.random.fold_in(stream_key, 6), position), (blocks,), jnp.float32, low / len(pieces), high / len(pieces))
        gain = gain * jnp.repeat(jnp.exp(draws), dims[position] // blocks).reshape((-1,) + (1,) * (len(dims) - 1 - position))
    return gain


def normal_values(own_key, shape, width, limit, split=(), kind=jnp.bfloat16):
    entries = width * jax.random.normal(own_key, shape, jnp.float32)
    if split:
        entries = entries * level_of(own_key, shape, split, -0.22, 0.18)
    return jnp.clip(entries, -limit, limit).astype(kind)


def noise_with(key, extent, scale, bound, split, heavy, kind=jnp.bfloat16):
    entries = scale * jax.random.normal(key, extent, jnp.float32)
    if split:
        entries = entries * level_of(key, extent, split, -0.22, 0.18)
    return jnp.clip(strengthened(entries, jax.random.fold_in(key, 3), *heavy), -bound, bound).astype(kind)


def setup_inputs(seed: int = 0) -> dict:
    key_list = jax.random.split(jax.random.key(seed), 6)
    features = normal_values(key_list[0], (SEQ_LEN, 3, C), 1.0, 6.0, ((0, 32), (2, 4)))
    short_taps = normal_values(key_list[1], (3, 3, C), 0.6, 4.0, ((2, 4),), jnp.float32)
    skip_gain = jnp.clip(0.5 + 1.0 * jax.random.uniform(key_list[2], (C,), jnp.float32) ** level_of(key_list[2], (C,), ((0, 4),), -0.2, 0.2), 0.5, 1.5)
    long_filter = normal_values(key_list[3], (SEQ_LEN, C), SEQ_LEN ** -0.5, 0.09375, ((0, 32), (1, 4)), jnp.float32)
    out_weight = noise_with(key_list[4], (C, D), C ** -0.5, 0.125, ((0, 4),), (0, 1, 4, 2.0))
    return dict(features=features, short_taps=short_taps, skip_gain=skip_gain, long_filter=long_filter, out_weight=out_weight)


def reference(features, short_taps, skip_gain, long_filter, out_weight):
    feats = features.astype(jnp.float32)
    padded = jnp.concatenate([jnp.zeros((2, 3, C), jnp.float32), feats], axis=0)
    mixed = short_taps[0] * padded[2:] + short_taps[1] * padded[1:-1] + short_taps[2] * padded[:-2]
    query = mixed[:, 0]
    product = mixed[:, 1] * mixed[:, 2]
    spectrum = jnp.fft.rfft(product, 2 * SEQ_LEN, axis=0) * jnp.fft.rfft(long_filter, 2 * SEQ_LEN, axis=0)
    conv = jnp.fft.irfft(spectrum, 2 * SEQ_LEN, axis=0)[:SEQ_LEN]
    gated = (query * (conv + skip_gain * product)).astype(jnp.bfloat16)
    blocks = gated.reshape(N_SEQ, TOK_DEV, C)
    group_width = C // N_CHAN

    def project(block_rows):
        total = jnp.zeros((TOK_DEV, D), jnp.float32)
        for group in range(N_CHAN):
            partial_out = jnp.dot(block_rows[:, group * group_width:(group + 1) * group_width],
                                  out_weight[group * group_width:(group + 1) * group_width],
                                  preferred_element_type=jnp.float32).astype(jnp.bfloat16)
            partial_out = lax.optimization_barrier(partial_out)
            total = total + partial_out.astype(jnp.float32)
        return total.astype(jnp.bfloat16)

    return lax.map(project, blocks).reshape(SEQ_LEN, D)
```

```python
import math

import jax
import jax.numpy as jnp
import ml_dtypes
import numpy as np
from jax import lax
from jax.experimental import pallas as pl
from jax.experimental.pallas import tpu as pltpu
from jax.sharding import PartitionSpec as P

GROUP = 16


def whole():
    return pl.BlockSpec(memory_space=pltpu.VMEM)


def transform_table(blocks, length):
    total = blocks * length
    k1 = np.arange(blocks)[:, None] + 0.25
    outer = 2.0 * math.pi * k1 * np.arange(blocks)[None, :] / blocks
    eye = np.eye(GROUP)
    ahead = np.concatenate([np.kron(np.cos(outer), eye), np.kron(-np.sin(outer), eye)], axis=0)
    back = np.concatenate([np.kron(np.cos(outer).T, eye), np.kron(-np.sin(outer).T, eye)], axis=0) / total
    inner = 2.0 * math.pi * np.outer(np.arange(length), np.arange(length)) / length
    cosine, sine = np.cos(inner), np.sin(inner)
    inner_ahead = np.concatenate([cosine, -sine, sine, cosine], axis=1)
    inner_back = np.concatenate([cosine, sine, -sine, cosine], axis=1)
    twist = 2.0 * math.pi * k1 * np.arange(length)[None, :] / total
    twist = np.concatenate([np.cos(twist), np.sin(twist)], axis=1).astype(np.float32)
    high = twist.astype(ml_dtypes.bfloat16)
    low = (twist - high.astype(np.float32)).astype(ml_dtypes.bfloat16)
    parts = [ahead, back, inner_ahead, inner_back, np.concatenate([high, low], axis=1)]
    return jnp.asarray(np.concatenate([part.astype(ml_dtypes.bfloat16) for part in parts], axis=0))


def read_table(table, blocks, length):
    size = blocks * GROUP
    at = 4 * size
    inner_ahead = jnp.concatenate([table[at : at + length, : 2 * length], table[at : at + length, 2 * length :]], axis=0)
    at += length
    inner_back = jnp.concatenate([table[at : at + length, : 2 * length], table[at : at + length, 2 * length :]], axis=0)
    at += length
    twist = table[at : at + blocks, :].astype(jnp.float32)
    twist = twist[:, : 2 * length] + twist[:, 2 * length :]
    spread = lambda part: jnp.broadcast_to(part[:, None, :], (blocks, GROUP, length)).reshape(size, length)
    return inner_ahead, inner_back, spread(twist[:, :length]), spread(twist[:, length:])


def start_all(pairs, sems):
    copies = [pltpu.make_async_copy(source, target, sems.at[i]) for i, (source, target) in enumerate(pairs)]
    for copy in copies:
        copy.start()
    return copies


def store_turned(target, first_row, value, start):
    parts, _, length = target.shape
    lanes = 1024 // parts // 2
    first = start % (parts * lanes) // lanes
    count = 128 // lanes
    row = first_row + start // (parts * lanes) * lanes
    turned = value.T.astype(jnp.bfloat16).reshape(count, lanes, length)
    target[first : first + count, row : row + lanes, :] = turned


def mixed(features, taps, slot, feature, columns):
    own = features[slot, :, columns].astype(jnp.float32)
    row = lax.broadcasted_iota(jnp.int32, own.shape, 0)
    one = jnp.where(row < 1, 0.0, pltpu.roll(own, 1, 0))
    two = jnp.where(row < 2, 0.0, pltpu.roll(own, 2, 0))
    tap = lambda lag: taps[lag, feature : feature + 1, columns]
    return tap(0) * own + tap(1) * one + tap(2) * two


def halo(prior, taps, feature, columns):
    row = lax.broadcasted_iota(jnp.int32, (8, 128), 0)
    before = prior[feature, :, columns].astype(jnp.float32)
    far, near = before[0:1], before[1:2]
    tap = lambda lag: taps[lag, feature : feature + 1, columns]
    first = tap(1) * near + tap(2) * far
    second = tap(2) * near
    return jnp.where(row == 0, first, 0.0) + jnp.where(row == 1, second, 0.0)


def whole_mixed(held, prior, taps, slot, feature, columns):
    value = mixed(held, taps, slot, feature, columns)
    return jnp.concatenate([value[0:8] + halo(prior, taps, feature, columns), value[8:]], axis=0)


def mix_kernel(features, taps, long_filter, prior, send, held, held_taps, held_filter, sems):
    width = held.shape[2]
    lanes = send.shape[1] // 2
    copies = start_all(
        [(long_filter, held_filter), (taps, held_taps), (features.at[1], held.at[0]), (features.at[2], held.at[1])],
        sems,
    )
    copies[0].wait()
    for start in range(0, width, 128):
        store_turned(send, lanes, held_filter[:, start : start + 128], start)
    for copy in copies[1:]:
        copy.wait()
    for start in range(0, width, 128):
        columns = slice(start, start + 128)
        product = whole_mixed(held, prior, held_taps, 0, 1, columns) * whole_mixed(
            held, prior, held_taps, 1, 2, columns
        )
        store_turned(send, 0, product, start)


def table_kernel(token, table, out, sems):
    del token
    start_all([(table, out)], sems)[0].wait()


def stage_kernel(where, token, weight, features, taps, skip, prior, query, direct, chunk, held, held_taps, held_skip, sems):
    del token
    width = query.shape[1]
    copies = start_all([(taps, held_taps), (skip, held_skip), (features, held)], sems)
    pieces = fetch_chunk(weight, where[0], chunk, sems, 3)
    for copy in copies:
        copy.wait()
    for start in range(0, width, 128):
        columns = slice(start, start + 128)
        part = [whole_mixed(held, prior, held_taps, i, i, columns) for i in range(3)]
        query[:, columns] = part[0]
        direct[:, columns] = held_skip[:, columns] * (part[1] * part[2])
    for copy in pieces:
        copy.wait()


def spectrum(received, table, first, inner_ahead, cosine, sine):
    blocks, _, length = received.shape
    size = blocks * GROUP
    group = lambda row: received[:, row : row + GROUP, :].reshape(size, length)
    signal = jnp.concatenate([group(first), group(first + GROUP)], axis=1)
    both = jnp.dot(table[: 2 * size, :], signal, preferred_element_type=jnp.float32)
    result = []
    for columns in (slice(0, length), slice(length, 2 * length)):
        real, imag = both[:size, columns], both[size:, columns]
        turned = jnp.concatenate([real * cosine + imag * sine, imag * cosine - real * sine], axis=1)
        result.append(jnp.dot(turned.astype(jnp.bfloat16), inner_ahead, preferred_element_type=jnp.float32))
    return result


def conv_kernel(table, received, out):
    blocks, rows, length = received.shape
    lanes = rows // 2
    size = blocks * GROUP
    inner_ahead, inner_back, cosine, sine = read_table(table, blocks, length)
    reals, imags = [], []
    signal_parts = spectrum(received, table, 0, inner_ahead, cosine, sine)
    filter_parts = spectrum(received, table, lanes, inner_ahead, cosine, sine)
    for part, other in zip(signal_parts, filter_parts):
        xr, xi = part[:, :length], part[:, length:]
        hr, hi = other[:, :length], other[:, length:]
        joined = jnp.concatenate([xr * hr - xi * hi, xr * hi + xi * hr], axis=1)
        both = jnp.dot(joined.astype(jnp.bfloat16), inner_back, preferred_element_type=jnp.float32)
        real, imag = both[:, :length], both[:, length:]
        reals.append((real * cosine - imag * sine).astype(jnp.bfloat16))
        imags.append((real * sine + imag * cosine).astype(jnp.bfloat16))
    both = jnp.dot(table[2 * size : 3 * size, :], jnp.concatenate(reals, axis=1), preferred_element_type=jnp.float32)
    both += jnp.dot(table[3 * size : 4 * size, :], jnp.concatenate(imags, axis=1), preferred_element_type=jnp.float32)
    for i in range(lanes // GROUP):
        part = both[:, i * length : (i + 1) * length].astype(jnp.bfloat16)
        out[:, i * GROUP : (i + 1) * GROUP, :] = part.reshape(blocks, GROUP, length)


PIECE = 256


def fetch_chunk(weight, index, held, sems, first_sem):
    depth, size = held.shape
    copies = []
    for piece in range(depth // PIECE):
        rows = pl.ds(piece * PIECE, PIECE)
        columns = pl.ds(pl.multiple_of(index * size, size), size)
        copy = pltpu.make_async_copy(weight.at[rows, columns], held.at[rows], sems.at[first_sem + piece])
        copy.start()
        copies.append(copy)
    return copies


def project(gated, held, copies):
    total = None
    for piece, copy in enumerate(copies):
        copy.wait()
        rows = slice(piece * PIECE, (piece + 1) * PIECE)
        part = jnp.dot(gated[:, rows], held[rows, :], preferred_element_type=jnp.float32)
        total = part if total is None else total + part
    return total


def far_kernel(query, direct, chunk, conv, gated_out, first_out, second_out):
    length, width = query.shape
    parts, lanes, _ = conv.shape
    half = lanes // 2
    count = 128 // half
    for start in range(0, width, 128):
        columns = slice(start, start + 128)
        first = start % (parts * half) // half
        row = start // (parts * half) * half
        turned = conv[first : first + count, row : row + half, :].reshape(128, length).astype(jnp.float32).T
        gated_out[:, columns] = (query[:, columns] * (turned + direct[:, columns])).astype(jnp.bfloat16)
    part = jnp.dot(gated_out[...], chunk[...], preferred_element_type=jnp.float32)
    top = length // 2
    first_out[...] = part[:top].astype(jnp.bfloat16)
    second_out[...] = part[top:].astype(jnp.bfloat16)


def near_kernel(where, weight, gated, ahead_held, ahead_out, behind_out, behind_held, held, sems):
    half = ahead_out.shape[0]
    count = held.shape[1] // PIECE
    ahead_pieces = fetch_chunk(weight, where[1], held.at[0], sems, 0)
    behind_pieces = fetch_chunk(weight, where[2], held.at[1], sems, count)
    part = project(gated, held.at[0], ahead_pieces)
    ahead_held[...] = part[:half].astype(jnp.bfloat16)
    ahead_out[...] = part[half:].astype(jnp.bfloat16)
    part = project(gated, held.at[1], behind_pieces)
    behind_out[...] = part[:half].astype(jnp.bfloat16)
    behind_held[...] = part[half:].astype(jnp.bfloat16)


def own_kernel(where, weight, gated, out, held, sems):
    out[...] = project(gated, held, fetch_chunk(weight, where[3], held, sems, 0))


def add_kernel(one, two, out):
    out[...] = (one[...].astype(jnp.float32) + two[...].astype(jnp.float32)).astype(jnp.bfloat16)


def last_kernel(own, first_one, first_two, second_one, second_two, out):
    half = out.shape[0] // 2
    wide = lambda ref: ref[...].astype(jnp.float32)
    out[:half] = (own[:half] + wide(first_one) + wide(first_two)).astype(jnp.bfloat16)
    out[half:] = (own[half:] + wide(second_one) + wide(second_two)).astype(jnp.bfloat16)


def call(kernel, outs, specs, name, scratch=(), out_specs=None, mebibytes=16):
    return pl.pallas_call(
        kernel,
        out_shape=outs,
        in_specs=specs,
        out_specs=jax.tree.map(lambda _: whole(), outs) if out_specs is None else out_specs,
        scratch_shapes=scratch,
        name=name,
        compiler_params=pltpu.CompilerParams(vmem_limit_bytes=mebibytes * 1024 * 1024),
    )


def shards(features, short_taps, skip_gain, long_filter, out_weight):
    length, width = long_filter.shape
    members = lax.axis_size("seq")
    groups = lax.axis_size("chan")
    lanes = width // members
    half = length // 2
    size = out_weight.shape[1] // groups
    bf16, f32 = jnp.bfloat16, jnp.float32
    shape = jax.ShapeDtypeStruct
    away = pl.BlockSpec(memory_space=pltpu.HBM)
    loose = pl.BlockSpec(memory_space=pl.ANY)
    scalar = pl.BlockSpec(memory_space=pltpu.SMEM)
    inside = whole()
    plain = shape((length, width), f32)
    turned_shape = shape((members, lanes, length), bf16)
    vmem = lambda dims, dtype: pltpu.VMEM(dims, dtype)
    flags = lambda count: pltpu.SemaphoreType.DMA((count,))

    prior = lax.ppermute(features[length - 2 :], "seq", [(i, i + 1) for i in range(members - 1)])
    prior = jnp.transpose(prior, (1, 0, 2))
    by_feature = jnp.transpose(features, (1, 0, 2))
    skip = skip_gain[None]
    send = call(
        mix_kernel,
        shape((members, 2 * lanes, length), bf16),
        [away] * 3 + [inside],
        "mix",
        [vmem((2, length, width), bf16), vmem(short_taps.shape, f32), vmem((length, width), f32), flags(4)],
        mebibytes=60,
    )(by_feature, short_taps, long_filter, prior)
    received = lax.all_to_all(send, "seq", 0, 0, tiled=True)
    table = transform_table(members, length)
    table = call(table_kernel, shape(table.shape, bf16), [loose, away], "table", [flags(1)])(send, table)
    spectral = call(conv_kernel, turned_shape, [inside] * 2, "conv")(table, received)
    conv = lax.all_to_all(spectral, "seq", 0, 0, tiled=True)

    side = lax.axis_index("seq") % 2
    me = lax.axis_index("chan")
    step = 1 - 2 * side
    where = jnp.stack([me + 2, me + step, me - step, me]).astype(jnp.int32) % groups

    def route(sign):
        pairs = []
        for s in range(members):
            for c in range(groups):
                move = sign * (1 - 2 * (s % 2))
                pairs.append((s * groups + c, s * groups + (c + move) % groups))
        return pairs

    def ahead(value):
        return lax.ppermute(value, ("seq", "chan"), route(1))

    def behind(value):
        return lax.ppermute(value, ("seq", "chan"), route(-1))

    part = shape((half, size), bf16)
    chunk = vmem((width, size), bf16)
    pieces = width // PIECE
    query, direct, far_chunk = call(
        stage_kernel,
        (plain, plain, shape((width, size), bf16)),
        [scalar, loose] + [away] * 4 + [inside],
        "stage",
        [vmem((3, length, width), bf16), vmem(short_taps.shape, f32), vmem(skip.shape, f32), flags(3 + pieces)],
        mebibytes=48,
    )(where, spectral, out_weight, by_feature, short_taps, skip, prior)
    gated, far_first, far_second = call(
        far_kernel, (shape((length, width), bf16), part, part), [inside] * 4, "far"
    )(query, direct, far_chunk, conv)
    got_first = ahead(far_first)
    got_second = behind(far_second)
    ahead_held, ahead_out, behind_out, behind_held = call(
        near_kernel,
        (part,) * 4,
        [scalar, away, inside],
        "near",
        [vmem((2, width, size), bf16), flags(2 * pieces)],
        mebibytes=48,
    )(where, out_weight, gated)
    ahead_got = ahead(ahead_out)
    behind_got = behind(behind_out)
    own = call(
        own_kernel, shape((length, size), f32), [scalar, away, inside], "own", [chunk, flags(pieces)], mebibytes=48
    )(where, out_weight, gated)
    first_got = ahead(call(add_kernel, part, [inside] * 2, "add_first")(got_first, ahead_held))
    second_got = behind(call(add_kernel, part, [inside] * 2, "add_second")(got_second, behind_held))
    return call(last_kernel, shape((length, size), bf16), [inside] * 5, "last")(
        own, first_got, behind_got, ahead_got, second_got
    )


def solution(mesh):
    in_specs = (
        P("seq", None, "chan"),
        P(None, None, "chan"),
        P("chan"),
        P("seq", "chan"),
        P("chan", None),
    )
    out_specs = P("seq", "chan")
    return jax.shard_map(shards, mesh=mesh, in_specs=in_specs, out_specs=out_specs, check_vma=False)
```

```python
import math

import jax
import jax.numpy as jnp
import ml_dtypes
import numpy as np
from jax import lax
from jax.experimental import pallas as pl
from jax.experimental.pallas import tpu as pltpu
from jax.sharding import PartitionSpec as P

GROUP = 8
TILE = 16


def whole():
    return pl.BlockSpec(memory_space=pltpu.VMEM)


def transform_table(blocks, length):
    total = blocks * length
    k1 = np.arange(blocks)[:, None] + 0.25
    outer = 2.0 * math.pi * k1 * np.arange(blocks)[None, :] / blocks
    eye = np.eye(GROUP)
    ahead = np.concatenate([np.kron(np.cos(outer), eye), np.kron(-np.sin(outer), eye)], axis=0)
    back = np.concatenate([np.kron(np.cos(outer).T, eye), np.kron(-np.sin(outer).T, eye)], axis=0) / total
    inner = 2.0 * math.pi * np.outer(np.arange(length), np.arange(length)) / length
    cosine, sine = np.cos(inner), np.sin(inner)
    inner_ahead = np.block([[cosine, -sine], [sine, cosine]])
    inner_back = np.block([[cosine, sine], [-sine, cosine]])
    twist = 2.0 * math.pi * k1 * np.arange(length)[None, :] / total
    twist = np.concatenate([np.cos(twist), np.sin(twist)], axis=1).astype(np.float32)
    high = twist.astype(ml_dtypes.bfloat16)
    low = (twist - high.astype(np.float32)).astype(ml_dtypes.bfloat16)
    parts = [ahead, back, inner_ahead, inner_back, high, low]
    return jnp.asarray(np.concatenate([part.astype(ml_dtypes.bfloat16) for part in parts], axis=0))


def read_table(table, blocks, length):
    size = blocks * GROUP
    at = 4 * size + 4 * length
    twist = table[at : at + blocks, :].astype(jnp.float32) + table[at + blocks : at + 2 * blocks, :].astype(jnp.float32)
    spread = lambda part: jnp.broadcast_to(part[:, None, :], (blocks, GROUP, length)).reshape(size, length)
    return (
        table[: 2 * size, :],
        (table[2 * size : 3 * size, :], table[3 * size : 4 * size, :]),
        table[4 * size : 4 * size + 2 * length, :],
        table[4 * size + 2 * length : at, :],
        spread(twist[:, :length]),
        spread(twist[:, length:]),
    )


def start_all(pairs, sems):
    copies = [pltpu.make_async_copy(source, target, sems.at[i]) for i, (source, target) in enumerate(pairs)]
    for copy in copies:
        copy.start()
    return copies


def store_turned(target, first_row, value, start):
    parts, _, length = target.shape
    lanes = 1024 // parts // 2
    first = start % (parts * lanes) // lanes
    count = 128 // lanes
    row = first_row + start // (parts * lanes) * lanes
    turned = value.T.astype(jnp.bfloat16).reshape(count, lanes, length)
    target[first : first + count, row : row + lanes, :] = turned


def mixed(features, taps, slot, feature, columns):
    own = features[slot, :, columns].astype(jnp.float32)
    row = lax.broadcasted_iota(jnp.int32, own.shape, 0)
    one = jnp.where(row < 1, 0.0, pltpu.roll(own, 1, 0))
    two = jnp.where(row < 2, 0.0, pltpu.roll(own, 2, 0))
    tap = lambda lag: taps[lag, feature : feature + 1, columns]
    return tap(0) * own + tap(1) * one + tap(2) * two


def halo(prior, taps, feature, columns):
    row = lax.broadcasted_iota(jnp.int32, (8, 128), 0)
    before = prior[feature, :, columns].astype(jnp.float32)
    far, near = before[14:15], before[15:16]
    tap = lambda lag: taps[lag, feature : feature + 1, columns]
    first = tap(1) * near + tap(2) * far
    second = tap(2) * near
    return jnp.where(row == 0, first, 0.0) + jnp.where(row == 1, second, 0.0)


def whole_mixed(held, prior, taps, slot, feature, columns):
    value = mixed(held, taps, slot, feature, columns)
    return jnp.concatenate([value[0:8] + halo(prior, taps, feature, columns), value[8:]], axis=0)


def handed_on(held, taps, slot, feature, columns):
    tail = held[slot, held.shape[1] - 16 :, columns].astype(jnp.float32)[8:]
    row = lax.broadcasted_iota(jnp.int32, tail.shape, 0)
    tap = lambda lag: taps[lag, feature : feature + 1, columns]
    both = tap(1) * jnp.where(row == 0, pltpu.roll(tail, 1, 0), 0.0)
    return both + tap(2) * jnp.where(row < 2, pltpu.roll(tail, 2, 0), 0.0)


def mix_kernel(features, taps, long_filter, send, token, held, held_taps, held_filter, edges, sems):
    width = held.shape[2]
    half = width // 2
    parts, rows, length = send.shape
    lanes = 2 * (rows // 5)
    copies = start_all(
        [(long_filter, held_filter), (taps, held_taps), (features.at[1], held.at[0]), (features.at[2], held.at[1])],
        sems,
    )
    edges[...] = jnp.zeros_like(edges)
    token[...] = jnp.zeros_like(token)
    copies[0].wait()
    for start in range(0, width, 128):
        store_turned(send, lanes, held_filter[:, start : start + 128], start)
    for copy in copies[1:]:
        copy.wait()
    row = lax.broadcasted_iota(jnp.int32, (8, 128), 0)
    for start in range(0, width, 128):
        columns = slice(start, start + 128)
        key = mixed(held, held_taps, 0, 1, columns)
        value = mixed(held, held_taps, 1, 2, columns)
        store_turned(send, 0, key * value, start)
        stack = jnp.where(row < 2, key[0:8], pltpu.roll(value[0:8], 2, 0))
        later = jnp.where(
            row < 2,
            handed_on(held, held_taps, 0, 1, columns),
            pltpu.roll(handed_on(held, held_taps, 1, 2, columns), 2, 0),
        )
        stack = jnp.where(row < 4, stack, pltpu.roll(later, 4, 0))
        top = start // half * 8
        edges[top : top + 8, start % half : start % half + 128] = stack
    for start in range(0, half, 128):
        first = start // (half // parts)
        count = 128 // (half // parts)
        turned = edges[:, start : start + 128].T.astype(jnp.bfloat16).reshape(count, half // parts, length)
        send[first : first + count, 2 * lanes :, :] = turned


def tail_kernel(token, table, features, table_out, tail, sems):
    del token
    rows = tail.shape[1]
    pairs = [(table, table_out), (features.at[:, pl.ds(features.shape[1] - rows, rows), :], tail)]
    for copy in start_all(pairs, sems):
        copy.wait()


def terms_kernel(token, features, taps, skip, prior, query, direct, held, held_taps, held_skip, sems):
    del token
    width = query.shape[1]
    copies = start_all([(taps, held_taps), (skip, held_skip), (features, held)], sems)
    for copy in copies:
        copy.wait()
    for start in range(0, width, 128):
        columns = slice(start, start + 128)
        part = [whole_mixed(held, prior, held_taps, i, i, columns) for i in range(3)]
        query[:, columns] = part[0].astype(jnp.bfloat16)
        direct[:, columns] = (held_skip[:, columns] * (part[1] * part[2])).astype(jnp.bfloat16)


def rows_of(received, row):
    blocks, _, length = received.shape
    return received[:, row : row + TILE, :].reshape(blocks * TILE, length).astype(jnp.float32)


def split_groups(rows, blocks):
    length = rows.shape[1]
    rows = rows.reshape(blocks, TILE, length)
    cut = lambda first: rows[:, first : first + GROUP].reshape(blocks * GROUP, length).astype(jnp.bfloat16)
    return [cut(first) for first in range(0, TILE, GROUP)]


def patched(received, edge_row, index):
    signal = rows_of(received, index * TILE)
    edge = rows_of(received, edge_row)
    length = edge.shape[1]
    before = jnp.concatenate([jnp.zeros((TILE, length), jnp.float32), edge[:-TILE]], axis=0)
    joined = pltpu.roll(edge, (length - 8 * index) % length, 1) + pltpu.roll(before, length - 8 * index - 4, 1)
    whole_edge = joined * pltpu.roll(joined, length - 2, 1)
    lane = lax.broadcasted_iota(jnp.int32, edge.shape, 1)
    return jnp.where(lane < 2, whole_edge, signal)


def spectrum(groups, ahead, inner_ahead, cosine, sine):
    size, length = groups[0].shape
    both = jnp.dot(ahead, jnp.concatenate(groups, axis=1), preferred_element_type=jnp.float32)
    turned = []
    for i in range(len(groups)):
        real, imag = both[:size, i * length : (i + 1) * length], both[size:, i * length : (i + 1) * length]
        turned.append(jnp.concatenate([real * cosine + imag * sine, imag * cosine - real * sine], axis=1))
    turned = jnp.concatenate(turned, axis=0).astype(jnp.bfloat16)
    return jnp.dot(turned, inner_ahead, preferred_element_type=jnp.float32)


def conv_kernel(token, table, received, out):
    del token
    blocks, lanes, length = out.shape
    size = blocks * GROUP
    tiles = lanes // TILE
    ahead, (back_real, back_imag), inner_ahead, inner_back, cosine, sine = read_table(table, blocks, length)
    groups = []
    for i in range(tiles):
        groups += split_groups(rows_of(received, lanes + i * TILE), blocks)
    other = spectrum(groups, ahead, inner_ahead, cosine, sine)
    groups = []
    for i in range(tiles):
        groups += split_groups(patched(received, 2 * lanes, i), blocks)
    part = spectrum(groups, ahead, inner_ahead, cosine, sine)
    xr, xi, hr, hi = part[:, :length], part[:, length:], other[:, :length], other[:, length:]
    joined = jnp.concatenate([xr * hr - xi * hi, xr * hi + xi * hr], axis=1)
    both = jnp.dot(joined.astype(jnp.bfloat16), inner_back, preferred_element_type=jnp.float32)
    reals, imags = [], []
    for i in range(len(groups)):
        real, imag = both[i * size : (i + 1) * size, :length], both[i * size : (i + 1) * size, length:]
        reals.append((real * cosine - imag * sine).astype(jnp.bfloat16))
        imags.append((real * sine + imag * cosine).astype(jnp.bfloat16))
    both = jnp.dot(back_real, jnp.concatenate(reals, axis=1), preferred_element_type=jnp.float32)
    both += jnp.dot(back_imag, jnp.concatenate(imags, axis=1), preferred_element_type=jnp.float32)
    for i in range(tiles):
        pair = []
        for j in range(i * TILE // GROUP, (i + 1) * TILE // GROUP):
            pair.append(both[:, j * length : (j + 1) * length].reshape(blocks, GROUP, length))
        out[:, i * TILE : (i + 1) * TILE, :] = jnp.concatenate(pair, axis=1).astype(jnp.bfloat16)


PIECE = 256


def fetch_chunk(weight, index, held, sems, first_sem):
    depth, size = held.shape
    copies = []
    for piece in range(depth // PIECE):
        rows = pl.ds(piece * PIECE, PIECE)
        columns = pl.ds(pl.multiple_of(index * size, size), size)
        copy = pltpu.make_async_copy(weight.at[rows, columns], held.at[rows], sems.at[first_sem + piece])
        copy.start()
        copies.append(copy)
    return copies


def project(gated, held, copies):
    total = None
    for piece, copy in enumerate(copies):
        copy.wait()
        rows = slice(piece * PIECE, (piece + 1) * PIECE)
        part = jnp.dot(gated[:, rows], held[rows, :], preferred_element_type=jnp.float32)
        total = part if total is None else total + part
    return total


def far_kernel(where, weight, query, direct, conv, gated_out, first_out, second_out, held, sems):
    length, width = query.shape
    parts, lanes, _ = conv.shape
    half = lanes // 2
    count = 128 // half
    pieces = fetch_chunk(weight, where[0], held, sems, 0)
    for start in range(0, width, 128):
        columns = slice(start, start + 128)
        first = start % (parts * half) // half
        row = start // (parts * half) * half
        turned = conv[first : first + count, row : row + half, :].reshape(128, length).astype(jnp.float32).T
        turned += direct[:, columns].astype(jnp.float32)
        gated_out[:, columns] = (query[:, columns].astype(jnp.float32) * turned).astype(jnp.bfloat16)
    part = project(gated_out, held, pieces)
    top = length // 2
    first_out[...] = part[:top].astype(jnp.bfloat16)
    second_out[...] = part[top:].astype(jnp.bfloat16)


def near_kernel(where, weight, gated, ahead_held, ahead_out, behind_out, behind_held, held, sems):
    half = ahead_out.shape[0]
    count = held.shape[1] // PIECE
    ahead_pieces = fetch_chunk(weight, where[1], held.at[0], sems, 0)
    behind_pieces = fetch_chunk(weight, where[2], held.at[1], sems, count)
    part = project(gated, held.at[0], ahead_pieces)
    ahead_held[...] = part[:half].astype(jnp.bfloat16)
    ahead_out[...] = part[half:].astype(jnp.bfloat16)
    part = project(gated, held.at[1], behind_pieces)
    behind_out[...] = part[:half].astype(jnp.bfloat16)
    behind_held[...] = part[half:].astype(jnp.bfloat16)


def own_kernel(where, weight, gated, out, held, sems):
    out[...] = project(gated, held, fetch_chunk(weight, where[3], held, sems, 0))


def add_kernel(one, two, out):
    out[...] = (one[...].astype(jnp.float32) + two[...].astype(jnp.float32)).astype(jnp.bfloat16)


def last_kernel(own, first_one, first_two, second_one, second_two, out):
    half = out.shape[0] // 2
    wide = lambda ref: ref[...].astype(jnp.float32)
    out[:half] = (own[:half] + wide(first_one) + wide(first_two)).astype(jnp.bfloat16)
    out[half:] = (own[half:] + wide(second_one) + wide(second_two)).astype(jnp.bfloat16)


def call(kernel, outs, specs, name, scratch=(), out_specs=None, mebibytes=16):
    return pl.pallas_call(
        kernel,
        out_shape=outs,
        in_specs=specs,
        out_specs=jax.tree.map(lambda _: whole(), outs) if out_specs is None else out_specs,
        scratch_shapes=scratch,
        name=name,
        compiler_params=pltpu.CompilerParams(vmem_limit_bytes=mebibytes * 1024 * 1024),
    )


def shards(features, short_taps, skip_gain, long_filter, out_weight):
    length, width = long_filter.shape
    members = lax.axis_size("seq")
    groups = lax.axis_size("chan")
    lanes = width // members
    half = length // 2
    size = out_weight.shape[1] // groups
    bf16, f32 = jnp.bfloat16, jnp.float32
    shape = jax.ShapeDtypeStruct
    away = pl.BlockSpec(memory_space=pltpu.HBM)
    loose = pl.BlockSpec(memory_space=pl.ANY)
    scalar = pl.BlockSpec(memory_space=pltpu.SMEM)
    inside = whole()
    terms = shape((length, width), bf16)
    turned_shape = shape((members, lanes, length), bf16)
    vmem = lambda dims, dtype: pltpu.VMEM(dims, dtype)
    flags = lambda count: pltpu.SemaphoreType.DMA((count,))

    by_feature = jnp.transpose(features, (1, 0, 2))
    skip = skip_gain[None]
    sending = shape((members, 2 * lanes + lanes // 2, length), bf16)
    send, token = call(
        mix_kernel,
        (sending, shape((8, 128), f32)),
        [away] * 3,
        "mix",
        [
            vmem((2, length, width), bf16),
            vmem(short_taps.shape, f32),
            vmem((length, width), f32),
            vmem((length, width // 2), f32),
            flags(4),
        ],
        mebibytes=60,
    )(by_feature, short_taps, long_filter)
    received = lax.all_to_all(send, "seq", 0, 0, tiled=True)
    table = transform_table(members, length)
    table, tail = call(
        tail_kernel,
        (shape(table.shape, bf16), shape((3, TILE, width), bf16)),
        [inside, away, away],
        "tail",
        [flags(2)],
        mebibytes=50,
    )(token, table, by_feature)
    prior = lax.ppermute(tail, "seq", [(i, i + 1) for i in range(members - 1)])
    spectral = call(conv_kernel, turned_shape, [loose] + [inside] * 2, "conv")(prior, table, received)
    conv = lax.all_to_all(spectral, "seq", 0, 0, tiled=True)

    side = lax.axis_index("seq") % 2
    me = lax.axis_index("chan")
    step = 1 - 2 * side
    where = jnp.stack([me + 2, me + step, me - step, me]).astype(jnp.int32) % groups

    def route(sign):
        pairs = []
        for s in range(members):
            for c in range(groups):
                move = sign * (1 - 2 * (s % 2))
                pairs.append((s * groups + c, s * groups + (c + move) % groups))
        return pairs

    def ahead(value):
        return lax.ppermute(value, ("seq", "chan"), route(1))

    def behind(value):
        return lax.ppermute(value, ("seq", "chan"), route(-1))

    part = shape((half, size), bf16)
    chunk = vmem((width, size), bf16)
    pieces = width // PIECE
    query, direct = call(
        terms_kernel,
        (terms, terms),
        [loose] + [away] * 3 + [inside],
        "terms",
        [vmem((3, length, width), bf16), vmem(short_taps.shape, f32), vmem(skip.shape, f32), flags(3)],
        mebibytes=50,
    )(spectral, by_feature, short_taps, skip, prior)
    gated, far_first, far_second = call(
        far_kernel,
        (shape((length, width), bf16), part, part),
        [scalar, away] + [inside] * 3,
        "far",
        [chunk, flags(pieces)],
        mebibytes=52,
    )(where, out_weight, query, direct, conv)
    got_first = ahead(far_first)
    got_second = behind(far_second)
    ahead_held, ahead_out, behind_out, behind_held = call(
        near_kernel,
        (part,) * 4,
        [scalar, away, inside],
        "near",
        [vmem((2, width, size), bf16), flags(2 * pieces)],
        mebibytes=48,
    )(where, out_weight, gated)
    ahead_got = ahead(ahead_out)
    behind_got = behind(behind_out)
    own = call(
        own_kernel, shape((length, size), f32), [scalar, away, inside], "own", [chunk, flags(pieces)], mebibytes=48
    )(where, out_weight, gated)
    first_got = ahead(call(add_kernel, part, [inside] * 2, "add_first")(got_first, ahead_held))
    second_got = behind(call(add_kernel, part, [inside] * 2, "add_second")(got_second, behind_held))
    return call(last_kernel, shape((length, size), bf16), [inside] * 5, "last")(
        own, first_got, behind_got, ahead_got, second_got
    )


def solution(mesh):
    in_specs = (
        P("seq", None, "chan"),
        P(None, None, "chan"),
        P("chan"),
        P("seq", "chan"),
        P("chan", None),
    )
    out_specs = P("seq", "chan")
    return jax.shard_map(shards, mesh=mesh, in_specs=in_specs, out_specs=out_specs, check_vma=False)
```

```python
import math

import jax
import jax.numpy as jnp
import ml_dtypes
import numpy as np
from jax import lax
from jax.experimental import pallas as pl
from jax.experimental.pallas import tpu as pltpu
from jax.sharding import PartitionSpec as P

GROUP = 8
TILE = 16


def whole():
    return pl.BlockSpec(memory_space=pltpu.VMEM)


def transform_table(blocks, length):
    total = blocks * length
    k1 = np.arange(blocks)[:, None] + 0.25
    outer = 2.0 * math.pi * k1 * np.arange(blocks)[None, :] / blocks
    eye = np.eye(GROUP)
    ahead = np.concatenate([np.kron(np.cos(outer), eye), np.kron(-np.sin(outer), eye)], axis=0)
    back = np.concatenate([np.kron(np.cos(outer).T, eye), np.kron(-np.sin(outer).T, eye)], axis=0) / total
    inner = 2.0 * math.pi * np.outer(np.arange(length), np.arange(length)) / length
    cosine, sine = np.cos(inner), np.sin(inner)
    inner_ahead = np.block([[cosine, -sine], [sine, cosine]])
    inner_back = np.block([[cosine, sine], [-sine, cosine]])
    twist = 2.0 * math.pi * k1 * np.arange(length)[None, :] / total
    twist = np.concatenate([np.cos(twist), np.sin(twist)], axis=1).astype(np.float32)
    high = twist.astype(ml_dtypes.bfloat16)
    low = (twist - high.astype(np.float32)).astype(ml_dtypes.bfloat16)
    parts = [ahead, back, inner_ahead, inner_back, high, low]
    return jnp.asarray(np.concatenate([part.astype(ml_dtypes.bfloat16) for part in parts], axis=0))


def read_table(table, blocks, length):
    size = blocks * GROUP
    at = 4 * size + 4 * length
    twist = table[at : at + blocks, :].astype(jnp.float32) + table[at + blocks : at + 2 * blocks, :].astype(jnp.float32)
    spread = lambda part: jnp.broadcast_to(part[:, None, :], (blocks, GROUP, length)).reshape(size, length)
    return (
        table[: 2 * size, :],
        (table[2 * size : 3 * size, :], table[3 * size : 4 * size, :]),
        table[4 * size : 4 * size + 2 * length, :],
        table[4 * size + 2 * length : at, :],
        spread(twist[:, :length]),
        spread(twist[:, length:]),
    )


def start_all(pairs, sems):
    copies = [pltpu.make_async_copy(source, target, sems.at[i]) for i, (source, target) in enumerate(pairs)]
    for copy in copies:
        copy.start()
    return copies


def store_turned(target, first_row, value, start):
    parts, _, length = target.shape
    first = start % (parts * GROUP) // GROUP
    row = first_row + start // (parts * GROUP) * GROUP
    turned = value.T.reshape(128 // GROUP, GROUP, length).astype(jnp.bfloat16)
    target[first : first + 128 // GROUP, row : row + GROUP, :] = turned


def mixed(features, taps, slot, feature, columns):
    own = features[slot, :, columns].astype(jnp.float32)
    row = lax.broadcasted_iota(jnp.int32, own.shape, 0)
    one = jnp.where(row < 1, 0.0, pltpu.roll(own, 1, 0))
    two = jnp.where(row < 2, 0.0, pltpu.roll(own, 2, 0))
    tap = lambda lag: taps[lag, feature : feature + 1, columns]
    return tap(0) * own + tap(1) * one + tap(2) * two


def halo(prior, taps, feature, columns):
    row = lax.broadcasted_iota(jnp.int32, (8, 128), 0)
    before = prior[feature, :, columns].astype(jnp.float32)
    far, near = before[0:1], before[1:2]
    tap = lambda lag: taps[lag, feature : feature + 1, columns]
    first = tap(1) * near + tap(2) * far
    second = tap(2) * near
    return jnp.where(row == 0, first, 0.0) + jnp.where(row == 1, second, 0.0)


def whole_mixed(held, prior, taps, slot, feature, columns):
    value = mixed(held, taps, slot, feature, columns)
    return jnp.concatenate([value[0:8] + halo(prior, taps, feature, columns), value[8:]], axis=0)


def handed_on(held, taps, slot, feature, columns):
    tail = held[slot, held.shape[1] - 16 :, columns].astype(jnp.float32)[8:]
    row = lax.broadcasted_iota(jnp.int32, tail.shape, 0)
    tap = lambda lag: taps[lag, feature : feature + 1, columns]
    both = tap(1) * jnp.where(row == 0, pltpu.roll(tail, 1, 0), 0.0)
    return both + tap(2) * jnp.where(row < 2, pltpu.roll(tail, 2, 0), 0.0)


def mix_kernel(features, taps, long_filter, send, token, held, held_taps, held_filter, edges, sems):
    width = held.shape[2]
    parts = send.shape[0]
    lanes = width // parts
    quarter = parts * GROUP
    copies = start_all(
        [(long_filter, held_filter), (taps, held_taps), (features.at[1], held.at[0]), (features.at[2], held.at[1])],
        sems,
    )
    edges[...] = jnp.zeros_like(edges)
    token[...] = jnp.zeros_like(token)
    copies[0].wait()
    for start in range(0, width, 128):
        store_turned(send, 0, held_filter[:, start : start + 128], start)
    for copy in copies[1:]:
        copy.wait()
    row = lax.broadcasted_iota(jnp.int32, (8, 128), 0)
    for start in range(0, width, 128):
        columns = slice(start, start + 128)
        key = mixed(held, held_taps, 0, 1, columns)
        value = mixed(held, held_taps, 1, 2, columns)
        store_turned(send, lanes, key * value, start)
        stack = jnp.where(row < 2, key[0:8], pltpu.roll(value[0:8], 2, 0))
        later = jnp.where(
            row < 2,
            handed_on(held, held_taps, 0, 1, columns),
            pltpu.roll(handed_on(held, held_taps, 1, 2, columns), 2, 0),
        )
        stack = jnp.where(row < 4, stack, pltpu.roll(later, 4, 0))
        top = start // quarter * 8
        edges[top : top + 8, start % quarter : start % quarter + 128] = stack
    for start in range(0, quarter, 128):
        store_turned(send, 2 * lanes, edges[:, start : start + 128], start)


def tail_kernel(token, table, features, table_out, tail, held, sems):
    del token
    rows = held.shape[1]
    pairs = [(table, table_out), (features.at[:, pl.ds(features.shape[1] - rows, rows), :], held)]
    for copy in start_all(pairs, sems):
        copy.wait()
    tail[...] = held[:, rows - tail.shape[1] :, :]


def terms_kernel(token, features, taps, skip, prior, query, direct, held, held_taps, held_skip, sems):
    del token
    width = query.shape[1]
    copies = start_all([(taps, held_taps), (skip, held_skip), (features, held)], sems)
    for copy in copies:
        copy.wait()
    for start in range(0, width, 128):
        columns = slice(start, start + 128)
        part = [whole_mixed(held, prior, held_taps, i, i, columns) for i in range(3)]
        query[:, columns] = part[0].astype(jnp.bfloat16)
        direct[:, columns] = (held_skip[:, columns] * (part[1] * part[2])).astype(jnp.bfloat16)


def rows_of(received, row):
    blocks, _, length = received.shape
    return received[:, row : row + GROUP, :].astype(jnp.float32).reshape(blocks * GROUP, length)


def patched(signal, edge, index):
    length = edge.shape[1]
    before = jnp.concatenate([jnp.zeros((GROUP, length), jnp.float32), edge[:-GROUP]], axis=0)
    joined = pltpu.roll(edge, (length - 8 * index) % length, 1) + pltpu.roll(before, length - 8 * index - 4, 1)
    whole_edge = joined * pltpu.roll(joined, length - 2, 1)
    lane = lax.broadcasted_iota(jnp.int32, edge.shape, 1)
    return jnp.where(lane < 2, whole_edge, signal)


def spectrum(groups, ahead, inner_ahead, cosine, sine):
    size, length = groups[0].shape
    both = jnp.dot(ahead, jnp.concatenate(groups, axis=1), preferred_element_type=jnp.float32)
    turned = []
    for i in range(len(groups)):
        real, imag = both[:size, i * length : (i + 1) * length], both[size:, i * length : (i + 1) * length]
        turned.append(jnp.concatenate([real * cosine + imag * sine, imag * cosine - real * sine], axis=1))
    turned = jnp.concatenate(turned, axis=0).astype(jnp.bfloat16)
    return jnp.dot(turned, inner_ahead, preferred_element_type=jnp.float32)


def conv_kernel(token, table, received, out):
    del token
    blocks, lanes, length = out.shape
    size = blocks * GROUP
    count = lanes // GROUP
    ahead, (back_real, back_imag), inner_ahead, inner_back, cosine, sine = read_table(table, blocks, length)
    groups = [rows_of(received, i * GROUP).astype(jnp.bfloat16) for i in range(count)]
    other = spectrum(groups, ahead, inner_ahead, cosine, sine)
    edge = rows_of(received, 2 * lanes)
    groups = [patched(rows_of(received, lanes + i * GROUP), edge, i).astype(jnp.bfloat16) for i in range(count)]
    part = spectrum(groups, ahead, inner_ahead, cosine, sine)
    xr, xi, hr, hi = part[:, :length], part[:, length:], other[:, :length], other[:, length:]
    joined = jnp.concatenate([xr * hr - xi * hi, xr * hi + xi * hr], axis=1)
    both = jnp.dot(joined.astype(jnp.bfloat16), inner_back, preferred_element_type=jnp.float32)
    reals, imags = [], []
    for i in range(len(groups)):
        real, imag = both[i * size : (i + 1) * size, :length], both[i * size : (i + 1) * size, length:]
        reals.append((real * cosine - imag * sine).astype(jnp.bfloat16))
        imags.append((real * sine + imag * cosine).astype(jnp.bfloat16))
    both = jnp.dot(back_real, jnp.concatenate(reals, axis=1), preferred_element_type=jnp.float32)
    both += jnp.dot(back_imag, jnp.concatenate(imags, axis=1), preferred_element_type=jnp.float32)
    for i in range(count):
        part = both[:, i * length : (i + 1) * length].reshape(blocks, GROUP, length)
        out[:, i * GROUP : (i + 1) * GROUP, :] = part.astype(jnp.bfloat16)


PIECE = 256


def chunk_index(kind, groups):
    step = 1 - 2 * (lax.axis_index("seq") % 2)
    return (lax.axis_index("chan") + (2, step, groups - step, 0)[kind]) % groups


def fetch_chunk(weight, index, held, sems, first_sem):
    depth, size = held.shape
    copies = []
    for piece in range(depth // PIECE):
        rows = pl.ds(piece * PIECE, PIECE)
        columns = pl.ds(pl.multiple_of(index * size, size), size)
        copy = pltpu.make_async_copy(weight.at[rows, columns], held.at[rows], sems.at[first_sem + piece])
        copy.start()
        copies.append(copy)
    return copies


def project(gated, held, copies):
    total = None
    for piece, copy in enumerate(copies):
        copy.wait()
        rows = slice(piece * PIECE, (piece + 1) * PIECE)
        part = jnp.dot(gated[:, rows], held[rows, :], preferred_element_type=jnp.float32)
        total = part if total is None else total + part
    return total


def far_kernel(weight, query, direct, conv, gated_out, first_out, second_out, held, sems):
    size = held.shape[1]
    length, width = query.shape
    quarter = conv.shape[0] * GROUP
    pieces = fetch_chunk(weight, chunk_index(0, weight.shape[1] // size), held, sems, 0)
    for start in range(0, width, 128):
        columns = slice(start, start + 128)
        first = start % quarter // GROUP
        row = start // quarter * GROUP
        turned = conv[first : first + 128 // GROUP, row : row + GROUP, :].astype(jnp.float32)
        turned = turned.reshape(128, length).T
        turned += direct[:, columns].astype(jnp.float32)
        gated_out[:, columns] = (query[:, columns].astype(jnp.float32) * turned).astype(jnp.bfloat16)
    part = project(gated_out, held, pieces)
    top = length // 2
    first_out[...] = part[:top].astype(jnp.bfloat16)
    second_out[...] = part[top:].astype(jnp.bfloat16)


def near_kernel(weight, gated, ahead_held, ahead_out, behind_out, behind_held, held, sems):
    half, size = ahead_out.shape
    count = held.shape[1] // PIECE
    ahead_pieces = fetch_chunk(weight, chunk_index(1, weight.shape[1] // size), held.at[0], sems, 0)
    behind_pieces = fetch_chunk(weight, chunk_index(2, weight.shape[1] // size), held.at[1], sems, count)
    part = project(gated, held.at[0], ahead_pieces)
    ahead_held[...] = part[:half].astype(jnp.bfloat16)
    ahead_out[...] = part[half:].astype(jnp.bfloat16)
    part = project(gated, held.at[1], behind_pieces)
    behind_out[...] = part[:half].astype(jnp.bfloat16)
    behind_held[...] = part[half:].astype(jnp.bfloat16)


def own_kernel(weight, gated, out, held, sems):
    size = held.shape[1]
    out[...] = project(gated, held, fetch_chunk(weight, chunk_index(3, weight.shape[1] // size), held, sems, 0))


def add_kernel(one, two, out):
    out[...] = (one[...].astype(jnp.float32) + two[...].astype(jnp.float32)).astype(jnp.bfloat16)


def last_kernel(own, first_one, first_two, second_one, second_two, out):
    half = out.shape[0] // 2
    wide = lambda ref: ref[...].astype(jnp.float32)
    out[:half] = (own[:half] + wide(first_one) + wide(first_two)).astype(jnp.bfloat16)
    out[half:] = (own[half:] + wide(second_one) + wide(second_two)).astype(jnp.bfloat16)


def call(kernel, outs, specs, name, scratch=(), out_specs=None, mebibytes=16):
    return pl.pallas_call(
        kernel,
        out_shape=outs,
        in_specs=specs,
        out_specs=jax.tree.map(lambda _: whole(), outs) if out_specs is None else out_specs,
        scratch_shapes=scratch,
        name=name,
        compiler_params=pltpu.CompilerParams(vmem_limit_bytes=mebibytes * 1024 * 1024),
    )


def shards(features, short_taps, skip_gain, long_filter, out_weight):
    length, width = long_filter.shape
    members = lax.axis_size("seq")
    groups = lax.axis_size("chan")
    lanes = width // members
    half = length // 2
    size = out_weight.shape[1] // groups
    bf16, f32 = jnp.bfloat16, jnp.float32
    shape = jax.ShapeDtypeStruct
    away = pl.BlockSpec(memory_space=pltpu.HBM)
    loose = pl.BlockSpec(memory_space=pl.ANY)
    inside = whole()
    terms = shape((length, width), bf16)
    turned_shape = shape((members, lanes, length), bf16)
    vmem = lambda dims, dtype: pltpu.VMEM(dims, dtype)
    flags = lambda count: pltpu.SemaphoreType.DMA((count,))

    by_feature = jnp.transpose(features, (1, 0, 2))
    skip = skip_gain[None]
    sending = shape((members, 2 * lanes + GROUP, length), bf16)
    send, token = call(
        mix_kernel,
        (sending, shape((8, 128), f32)),
        [away] * 3,
        "mix",
        [
            vmem((2, length, width), bf16),
            vmem(short_taps.shape, f32),
            vmem((length, width), f32),
            vmem((length, members * GROUP), f32),
            flags(4),
        ],
        mebibytes=60,
    )(by_feature, short_taps, long_filter)
    received = lax.all_to_all(send, "seq", 0, 0, tiled=True)
    table = transform_table(members, length)
    table, tail = call(
        tail_kernel,
        (shape(table.shape, bf16), shape((3, 2, width), bf16)),
        [inside, away, away],
        "tail",
        [vmem((3, TILE, width), bf16), flags(2)],
        mebibytes=50,
    )(token, table, by_feature)
    prior = lax.ppermute(tail, "seq", [(i, i + 1) for i in range(members - 1)])
    spectral = call(conv_kernel, turned_shape, [loose] + [inside] * 2, "conv")(prior, table, received)
    conv = lax.all_to_all(spectral, "seq", 0, 0, tiled=True)

    def route(sign):
        pairs = []
        for s in range(members):
            for c in range(groups):
                move = sign * (1 - 2 * (s % 2))
                pairs.append((s * groups + c, s * groups + (c + move) % groups))
        return pairs

    def ahead(value):
        return lax.ppermute(value, ("seq", "chan"), route(1))

    def behind(value):
        return lax.ppermute(value, ("seq", "chan"), route(-1))

    part = shape((half, size), bf16)
    chunk = vmem((width, size), bf16)
    pieces = width // PIECE
    query, direct = call(
        terms_kernel,
        (terms, terms),
        [loose] + [away] * 3 + [inside],
        "terms",
        [vmem((3, length, width), bf16), vmem(short_taps.shape, f32), vmem(skip.shape, f32), flags(3)],
        mebibytes=50,
    )(spectral, by_feature, short_taps, skip, prior)
    gated, far_first, far_second = call(
        far_kernel,
        (shape((length, width), bf16), part, part),
        [away] + [inside] * 3,
        "far",
        [chunk, flags(pieces)],
        mebibytes=52,
    )(out_weight, query, direct, conv)
    got_first = ahead(far_first)
    got_second = behind(far_second)
    ahead_held, ahead_out, behind_out, behind_held = call(
        near_kernel,
        (part,) * 4,
        [away, inside],
        "near",
        [vmem((2, width, size), bf16), flags(2 * pieces)],
        mebibytes=48,
    )(out_weight, gated)
    ahead_got = ahead(ahead_out)
    behind_got = behind(behind_out)
    own = call(
        own_kernel, shape((length, size), f32), [away, inside], "own", [chunk, flags(pieces)], mebibytes=48
    )(out_weight, gated)
    first_got = ahead(call(add_kernel, part, [inside] * 2, "add_first")(got_first, ahead_held))
    second_got = behind(call(add_kernel, part, [inside] * 2, "add_second")(got_second, behind_held))
    return call(last_kernel, shape((length, size), bf16), [inside] * 5, "last")(
        own, first_got, behind_got, ahead_got, second_got
    )


def solution(mesh):
    in_specs = (
        P("seq", None, "chan"),
        P(None, None, "chan"),
        P("chan"),
        P("seq", "chan"),
        P("chan", None),
    )
    out_specs = P("seq", "chan")
    return jax.shard_map(shards, mesh=mesh, in_specs=in_specs, out_specs=out_specs, check_vma=False)
```

```python
import functools
import math

import jax
import jax.numpy as jnp
import ml_dtypes
import numpy as np
from jax import lax
from jax.experimental import pallas as pl
from jax.experimental.pallas import tpu as pltpu
from jax.sharding import PartitionSpec as P

GROUP = 8
TILE = 16


def whole():
    return pl.BlockSpec(memory_space=pltpu.VMEM)


def transform_table(order, length):
    blocks = len(order)
    total = blocks * length
    k1 = np.arange(blocks)[:, None] + 0.25
    outer = 2.0 * math.pi * k1 * np.array(order)[None, :] / blocks
    eye = np.eye(GROUP)
    ahead = np.concatenate([np.kron(np.cos(outer), eye), np.kron(-np.sin(outer), eye)], axis=0)
    back = np.concatenate([np.kron(np.cos(outer).T, eye), np.kron(-np.sin(outer).T, eye)], axis=0) / total
    inner = 2.0 * math.pi * np.outer(np.arange(length), np.arange(length)) / length
    cosine, sine = np.cos(inner), np.sin(inner)
    inner_ahead = np.block([[cosine, -sine], [sine, cosine]])
    inner_back = np.block([[cosine, sine], [-sine, cosine]])
    twist = 2.0 * math.pi * k1 * np.arange(length)[None, :] / total
    twist = np.concatenate([np.cos(twist), np.sin(twist)], axis=1).astype(np.float32)
    high = twist.astype(ml_dtypes.bfloat16)
    low = (twist - high.astype(np.float32)).astype(ml_dtypes.bfloat16)
    parts = [ahead, back, inner_ahead, inner_back, high, low]
    return jnp.asarray(np.concatenate([part.astype(ml_dtypes.bfloat16) for part in parts], axis=0))


def read_table(table, blocks, length):
    size = blocks * GROUP
    at = 4 * size + 4 * length
    twist = table[at : at + blocks, :].astype(jnp.float32) + table[at + blocks : at + 2 * blocks, :].astype(jnp.float32)
    spread = lambda part: jnp.broadcast_to(part[:, None, :], (blocks, GROUP, length)).reshape(size, length)
    return (
        table[: 2 * size, :],
        (table[2 * size : 3 * size, :], table[3 * size : 4 * size, :]),
        table[4 * size : 4 * size + 2 * length, :],
        table[4 * size + 2 * length : at, :],
        spread(twist[:, :length]),
        spread(twist[:, length:]),
    )


def start_all(pairs, sems):
    copies = [pltpu.make_async_copy(source, target, sems.at[i]) for i, (source, target) in enumerate(pairs)]
    for copy in copies:
        copy.start()
    return copies


def store_turned(target, first_row, value, start):
    parts, _, length = target.shape
    first = start % (parts * GROUP) // GROUP
    row = first_row + start // (parts * GROUP) * GROUP
    turned = value.T.reshape(128 // GROUP, GROUP, length).astype(jnp.bfloat16)
    target[first : first + 128 // GROUP, row : row + GROUP, :] = turned


def mixed(features, taps, slot, feature, columns):
    own = features[slot, :, columns].astype(jnp.float32)
    row = lax.broadcasted_iota(jnp.int32, own.shape, 0)
    one = jnp.where(row < 1, 0.0, pltpu.roll(own, 1, 0))
    two = jnp.where(row < 2, 0.0, pltpu.roll(own, 2, 0))
    tap = lambda lag: taps[lag, feature : feature + 1, columns]
    return tap(0) * own + tap(1) * one + tap(2) * two


def halo(prior, taps, feature, columns):
    row = lax.broadcasted_iota(jnp.int32, (8, 128), 0)
    before = prior[feature, :, columns].astype(jnp.float32)
    far, near = before[0:1], before[1:2]
    tap = lambda lag: taps[lag, feature : feature + 1, columns]
    first = tap(1) * near + tap(2) * far
    second = tap(2) * near
    return jnp.where(row == 0, first, 0.0) + jnp.where(row == 1, second, 0.0)


def whole_mixed(held, prior, taps, slot, feature, columns):
    value = mixed(held, taps, slot, feature, columns)
    return jnp.concatenate([value[0:8] + halo(prior, taps, feature, columns), value[8:]], axis=0)


def handed_on(held, taps, slot, feature, columns):
    tail = held[slot, held.shape[1] - 16 :, columns].astype(jnp.float32)[8:]
    row = lax.broadcasted_iota(jnp.int32, tail.shape, 0)
    tap = lambda lag: taps[lag, feature : feature + 1, columns]
    both = tap(1) * jnp.where(row == 0, pltpu.roll(tail, 1, 0), 0.0)
    return both + tap(2) * jnp.where(row < 2, pltpu.roll(tail, 2, 0), 0.0)


def mix_kernel(features, taps, long_filter, send, token, held, held_taps, held_filter, edges, sems):
    width = held.shape[2]
    parts = send.shape[0]
    lanes = width // parts
    quarter = parts * GROUP
    copies = start_all(
        [(long_filter, held_filter), (taps, held_taps), (features.at[1], held.at[0]), (features.at[2], held.at[1])],
        sems,
    )
    edges[...] = jnp.zeros_like(edges)
    token[...] = jnp.zeros_like(token)
    copies[0].wait()
    for start in range(0, width, 128):
        store_turned(send, 0, held_filter[:, start : start + 128], start)
    for copy in copies[1:]:
        copy.wait()
    row = lax.broadcasted_iota(jnp.int32, (8, 128), 0)
    for start in range(0, width, 128):
        columns = slice(start, start + 128)
        key = mixed(held, held_taps, 0, 1, columns)
        value = mixed(held, held_taps, 1, 2, columns)
        store_turned(send, lanes, key * value, start)
        stack = jnp.where(row < 2, key[0:8], pltpu.roll(value[0:8], 2, 0))
        later = jnp.where(
            row < 2,
            handed_on(held, held_taps, 0, 1, columns),
            pltpu.roll(handed_on(held, held_taps, 1, 2, columns), 2, 0),
        )
        stack = jnp.where(row < 4, stack, pltpu.roll(later, 4, 0))
        top = start // quarter * 8
        edges[top : top + 8, start % quarter : start % quarter + 128] = stack
    for start in range(0, quarter, 128):
        store_turned(send, 2 * lanes, edges[:, start : start + 128], start)


def tail_kernel(token, table, features, table_out, tail, held, sems):
    del token
    rows = held.shape[1]
    pairs = [(table, table_out), (features.at[:, pl.ds(features.shape[1] - rows, rows), :], held)]
    for copy in start_all(pairs, sems):
        copy.wait()
    tail[...] = held[:, rows - tail.shape[1] :, :]


def terms_kernel(token, features, taps, skip, prior, query, direct, held, held_taps, held_skip, sems):
    del token
    width = query.shape[1]
    copies = start_all([(taps, held_taps), (skip, held_skip), (features, held)], sems)
    for copy in copies:
        copy.wait()
    for start in range(0, width, 128):
        columns = slice(start, start + 128)
        part = [whole_mixed(held, prior, held_taps, i, i, columns) for i in range(3)]
        query[:, columns] = part[0].astype(jnp.bfloat16)
        direct[:, columns] = (held_skip[:, columns] * (part[1] * part[2])).astype(jnp.bfloat16)


def rows_of(received, row):
    blocks, _, length = received.shape
    return received[:, row : row + GROUP, :].astype(jnp.float32).reshape(blocks * GROUP, length)


def patched(signal, edge, index, order):
    length = edge.shape[1]
    nothing = jnp.zeros((GROUP, length), jnp.float32)
    at = lambda block: edge[order.index(block) * GROUP : (order.index(block) + 1) * GROUP]
    before = jnp.concatenate([at(block - 1) if block else nothing for block in order], axis=0)
    joined = pltpu.roll(edge, (length - 8 * index) % length, 1) + pltpu.roll(before, length - 8 * index - 4, 1)
    whole_edge = joined * pltpu.roll(joined, length - 2, 1)
    lane = lax.broadcasted_iota(jnp.int32, edge.shape, 1)
    return jnp.where(lane < 2, whole_edge, signal)


def spectrum(groups, ahead, inner_ahead, cosine, sine):
    size, length = groups[0].shape
    both = jnp.dot(ahead, jnp.concatenate(groups, axis=1), preferred_element_type=jnp.float32)
    turned = []
    for i in range(len(groups)):
        real, imag = both[:size, i * length : (i + 1) * length], both[size:, i * length : (i + 1) * length]
        turned.append(jnp.concatenate([real * cosine + imag * sine, imag * cosine - real * sine], axis=1))
    turned = jnp.concatenate(turned, axis=0).astype(jnp.bfloat16)
    return jnp.dot(turned, inner_ahead, preferred_element_type=jnp.float32)


def conv_kernel(order, token, table, received, out):
    del token
    blocks, lanes, length = out.shape
    size = blocks * GROUP
    count = lanes // GROUP
    ahead, (back_real, back_imag), inner_ahead, inner_back, cosine, sine = read_table(table, blocks, length)
    groups = [rows_of(received, i * GROUP).astype(jnp.bfloat16) for i in range(count)]
    other = spectrum(groups, ahead, inner_ahead, cosine, sine)
    edge = rows_of(received, 2 * lanes)
    groups = [patched(rows_of(received, lanes + i * GROUP), edge, i, order).astype(jnp.bfloat16) for i in range(count)]
    part = spectrum(groups, ahead, inner_ahead, cosine, sine)
    xr, xi, hr, hi = part[:, :length], part[:, length:], other[:, :length], other[:, length:]
    joined = jnp.concatenate([xr * hr - xi * hi, xr * hi + xi * hr], axis=1)
    both = jnp.dot(joined.astype(jnp.bfloat16), inner_back, preferred_element_type=jnp.float32)
    reals, imags = [], []
    for i in range(len(groups)):
        real, imag = both[i * size : (i + 1) * size, :length], both[i * size : (i + 1) * size, length:]
        reals.append((real * cosine - imag * sine).astype(jnp.bfloat16))
        imags.append((real * sine + imag * cosine).astype(jnp.bfloat16))
    both = jnp.dot(back_real, jnp.concatenate(reals, axis=1), preferred_element_type=jnp.float32)
    both += jnp.dot(back_imag, jnp.concatenate(imags, axis=1), preferred_element_type=jnp.float32)
    for i in range(count):
        part = both[:, i * length : (i + 1) * length].reshape(blocks, GROUP, length)
        out[:, i * GROUP : (i + 1) * GROUP, :] = part.astype(jnp.bfloat16)


PIECE = 256


def chunk_start(kind, total):
    groups = lax.axis_size("chan")
    step = 1 - 2 * (lax.axis_index("seq") % 2)
    index = (lax.axis_index("chan") + (2, step, groups - step, 0)[kind]) % groups
    return index * (total // groups)


def fetch_columns(weight, first_column, held, sems, first_sem):
    depth, size = held.shape
    copies = []
    for piece in range(depth // PIECE):
        rows = pl.ds(piece * PIECE, PIECE)
        columns = pl.ds(pl.multiple_of(first_column, 128), size)
        copy = pltpu.make_async_copy(weight.at[rows, columns], held.at[rows], sems.at[first_sem + piece])
        copy.start()
        copies.append(copy)
    return copies


def project(gated, held, copies):
    total = None
    for piece, copy in enumerate(copies):
        copy.wait()
        rows = slice(piece * PIECE, (piece + 1) * PIECE)
        part = jnp.dot(gated[:, rows], held[rows, :], preferred_element_type=jnp.float32)
        total = part if total is None else total + part
    return total


def far_kernel(weight, query, direct, conv, gated_out, first_out, second_out, held, sems):
    length, width = query.shape
    quarter = conv.shape[0] * GROUP
    pieces = fetch_columns(weight, chunk_start(0, weight.shape[1]), held, sems, 0)
    for start in range(0, width, 128):
        columns = slice(start, start + 128)
        first = start % quarter // GROUP
        row = start // quarter * GROUP
        turned = conv[first : first + 128 // GROUP, row : row + GROUP, :].astype(jnp.float32)
        turned = turned.reshape(128, length).T
        turned += direct[:, columns].astype(jnp.float32)
        gated_out[:, columns] = (query[:, columns].astype(jnp.float32) * turned).astype(jnp.bfloat16)
    part = project(gated_out, held, pieces).astype(jnp.bfloat16)
    split = second_out.shape[1]
    second_out[...] = part[:, :split]
    first_out[...] = part[:, split:]


def near_kernel(weight, gated, ahead_out, behind_out, ahead_held, behind_held, sems):
    total = weight.shape[1]
    right = ahead_out.shape[1]
    behind_pieces = fetch_columns(weight, chunk_start(2, total) + right, behind_held, sems, 0)
    ahead_pieces = fetch_columns(weight, chunk_start(1, total), ahead_held, sems, len(behind_pieces))
    behind_out[...] = project(gated, behind_held, behind_pieces).astype(jnp.bfloat16)
    ahead_out[...] = project(gated, ahead_held, ahead_pieces).astype(jnp.bfloat16)


def joined_kernel(weight, gated, got, ahead_out, behind_out, ahead_held, behind_held, sems):
    total = weight.shape[1]
    left = behind_out.shape[1]
    behind_pieces = fetch_columns(weight, chunk_start(2, total), behind_held, sems, 0)
    ahead_pieces = fetch_columns(weight, chunk_start(1, total) + left, ahead_held, sems, len(behind_pieces))
    part = project(gated, behind_held, behind_pieces)
    behind_out[...] = (part + got[...].astype(jnp.float32)).astype(jnp.bfloat16)
    ahead_out[...] = project(gated, ahead_held, ahead_pieces).astype(jnp.bfloat16)


def own_kernel(weight, gated, out, held, sems):
    out[...] = project(gated, held, fetch_columns(weight, chunk_start(3, weight.shape[1]), held, sems, 0))


def add_kernel(one, two, out):
    out[...] = (one[...].astype(jnp.float32) + two[...].astype(jnp.float32)).astype(jnp.bfloat16)


def last_kernel(own, first_one, first_two, second_one, second_two, out):
    split = second_one.shape[1]
    wide = lambda ref: ref[...].astype(jnp.float32)
    out[:, :split] = (own[:, :split] + wide(second_one) + wide(second_two)).astype(jnp.bfloat16)
    out[:, split:] = (own[:, split:] + wide(first_one) + wide(first_two)).astype(jnp.bfloat16)


def call(kernel, outs, specs, name, scratch=(), out_specs=None, mebibytes=16):
    return pl.pallas_call(
        kernel,
        out_shape=outs,
        in_specs=specs,
        out_specs=jax.tree.map(lambda _: whole(), outs) if out_specs is None else out_specs,
        scratch_shapes=scratch,
        name=name,
        compiler_params=pltpu.CompilerParams(vmem_limit_bytes=mebibytes * 1024 * 1024),
    )


def shards(features, short_taps, skip_gain, long_filter, out_weight):
    length, width = long_filter.shape
    members = lax.axis_size("seq")
    groups = lax.axis_size("chan")
    lanes = width // members
    size = out_weight.shape[1] // groups
    bf16, f32 = jnp.bfloat16, jnp.float32
    shape = jax.ShapeDtypeStruct
    away = pl.BlockSpec(memory_space=pltpu.HBM)
    loose = pl.BlockSpec(memory_space=pl.ANY)
    inside = whole()
    terms = shape((length, width), bf16)
    turned_shape = shape((members, lanes, length), bf16)
    vmem = lambda dims, dtype: pltpu.VMEM(dims, dtype)
    flags = lambda count: pltpu.SemaphoreType.DMA((count,))

    head = 2 * members // 3
    order = [head] + [i for i in range(members) if i != head]

    def exchange(value):
        return lax.all_to_all(value, "seq", 0, 0, axis_index_groups=[order], tiled=True)

    by_feature = jnp.transpose(features, (1, 0, 2))
    skip = skip_gain[None]
    sending = shape((members, 2 * lanes + GROUP, length), bf16)
    send, token = call(
        mix_kernel,
        (sending, shape((8, 128), f32)),
        [away] * 3,
        "mix",
        [
            vmem((2, length, width), bf16),
            vmem(short_taps.shape, f32),
            vmem((length, width), f32),
            vmem((length, members * GROUP), f32),
            flags(4),
        ],
        mebibytes=60,
    )(by_feature, short_taps, long_filter)
    received = exchange(send)
    table = transform_table(order, length)
    table, tail = call(
        tail_kernel,
        (shape(table.shape, bf16), shape((3, 2, width), bf16)),
        [inside, away, away],
        "tail",
        [vmem((3, TILE, width), bf16), flags(2)],
        mebibytes=50,
    )(token, table, by_feature)
    prior = lax.ppermute(tail, "seq", [(i, i + 1) for i in range(members - 1)])
    spectral = call(functools.partial(conv_kernel, order), turned_shape, [loose] + [inside] * 2, "conv")(prior, table, received)
    conv = exchange(spectral)

    def route(sign):
        pairs = []
        for s in range(members):
            for c in range(groups):
                move = sign * (1 - 2 * (s % 2))
                pairs.append((s * groups + c, s * groups + (c + move) % groups))
        return pairs

    def ahead(value):
        return lax.ppermute(value, ("seq", "chan"), route(1))

    def behind(value):
        return lax.ppermute(value, ("seq", "chan"), route(-1))

    split = size // 2
    left, right = shape((length, split), bf16), shape((length, size - split), bf16)
    chunk = vmem((width, size), bf16)
    pieces = width // PIECE
    query, direct = call(
        terms_kernel,
        (terms, terms),
        [loose] + [away] * 3 + [inside],
        "terms",
        [vmem((3, length, width), bf16), vmem(short_taps.shape, f32), vmem(skip.shape, f32), flags(3)],
        mebibytes=50,
    )(spectral, by_feature, short_taps, skip, prior)
    gated, far_first, far_second = call(
        far_kernel,
        (shape((length, width), bf16), right, left),
        [away] + [inside] * 3,
        "far",
        [chunk, flags(pieces)],
        mebibytes=52,
    )(out_weight, query, direct, conv)
    got_first = ahead(far_first)
    got_second = behind(far_second)

    def pair(kernel, ahead_shape, behind_shape, name, *more):
        return call(
            kernel,
            (ahead_shape, behind_shape),
            [away] + [inside] * (1 + len(more)),
            name,
            [vmem((width, ahead_shape.shape[1]), bf16), vmem((width, behind_shape.shape[1]), bf16), flags(2 * pieces)],
            mebibytes=48,
        )(out_weight, gated, *more)

    ahead_out, behind_out = pair(near_kernel, left, right, "near")
    behind_got = behind(behind_out)
    ahead_got = ahead(ahead_out)
    ahead_held, joined = pair(joined_kernel, right, left, "joined", got_second)
    second_got = behind(joined)
    own = call(
        own_kernel, shape((length, size), f32), [away, inside], "own", [chunk, flags(pieces)], mebibytes=48
    )(out_weight, gated)
    first_got = ahead(call(add_kernel, right, [inside] * 2, "add")(got_first, ahead_held))
    return call(last_kernel, shape((length, size), bf16), [inside] * 5, "last")(
        own, first_got, behind_got, ahead_got, second_got
    )


def solution(mesh):
    in_specs = (
        P("seq", None, "chan"),
        P(None, None, "chan"),
        P("chan"),
        P("seq", "chan"),
        P("chan", None),
    )
    out_specs = P("seq", "chan")
    return jax.shard_map(shards, mesh=mesh, in_specs=in_specs, out_specs=out_specs, check_vma=False)
```

```python
import functools
import math

import jax
import jax.numpy as jnp
import ml_dtypes
import numpy as np
from jax import lax
from jax.experimental import pallas as pl
from jax.experimental.pallas import tpu as pltpu
from jax.sharding import PartitionSpec as P

GROUP = 8
TILE = 16


def whole():
    return pl.BlockSpec(memory_space=pltpu.VMEM)


def transform_table(order, length):
    blocks = len(order)
    total = blocks * length
    k1 = np.arange(blocks)[:, None] + 0.25
    outer = 2.0 * math.pi * k1 * np.array(order)[None, :] / blocks
    eye = np.eye(GROUP)
    ahead = np.concatenate([np.kron(np.cos(outer), eye), np.kron(-np.sin(outer), eye)], axis=0)
    back = np.concatenate([np.kron(np.cos(outer).T, eye), np.kron(-np.sin(outer).T, eye)], axis=0) / total
    inner = 2.0 * math.pi * np.outer(np.arange(length), np.arange(length)) / length
    cosine, sine = np.cos(inner), np.sin(inner)
    inner_ahead = np.block([[cosine, -sine], [sine, cosine]])
    inner_back = np.block([[cosine, sine], [-sine, cosine]])
    twist = 2.0 * math.pi * k1 * np.arange(length)[None, :] / total
    twist = np.concatenate([np.cos(twist), np.sin(twist)], axis=1).astype(np.float32)
    high = twist.astype(ml_dtypes.bfloat16)
    low = (twist - high.astype(np.float32)).astype(ml_dtypes.bfloat16)
    parts = [ahead, back, inner_ahead, inner_back, high, low]
    return jnp.asarray(np.concatenate([part.astype(ml_dtypes.bfloat16) for part in parts], axis=0))


def read_table(table, blocks, length):
    size = blocks * GROUP
    at = 4 * size + 4 * length
    twist = table[at : at + blocks, :].astype(jnp.float32) + table[at + blocks : at + 2 * blocks, :].astype(jnp.float32)
    spread = lambda part: jnp.broadcast_to(part[:, None, :], (blocks, GROUP, length)).reshape(size, length)
    return (
        table[: 2 * size, :],
        (table[2 * size : 3 * size, :], table[3 * size : 4 * size, :]),
        table[4 * size : 4 * size + 2 * length, :],
        table[4 * size + 2 * length : at, :],
        spread(twist[:, :length]),
        spread(twist[:, length:]),
    )


def start_all(pairs, sems):
    copies = [pltpu.make_async_copy(source, target, sems.at[i]) for i, (source, target) in enumerate(pairs)]
    for copy in copies:
        copy.start()
    return copies


def store_turned(target, first_row, value, start):
    parts, _, length = target.shape
    first = start % (parts * GROUP) // GROUP
    row = first_row + start // (parts * GROUP) * GROUP
    turned = value.T.reshape(128 // GROUP, GROUP, length).astype(jnp.bfloat16)
    target[first : first + 128 // GROUP, row : row + GROUP, :] = turned


def mixed(features, taps, slot, feature, columns):
    own = features[slot, :, columns].astype(jnp.float32)
    row = lax.broadcasted_iota(jnp.int32, own.shape, 0)
    one = jnp.where(row < 1, 0.0, pltpu.roll(own, 1, 0))
    two = jnp.where(row < 2, 0.0, pltpu.roll(own, 2, 0))
    tap = lambda lag: taps[lag, feature : feature + 1, columns]
    return tap(0) * own + tap(1) * one + tap(2) * two


def halo(prior, taps, feature, columns):
    row = lax.broadcasted_iota(jnp.int32, (8, 128), 0)
    before = prior[feature, :, columns].astype(jnp.float32)
    far, near = before[0:1], before[1:2]
    tap = lambda lag: taps[lag, feature : feature + 1, columns]
    first = tap(1) * near + tap(2) * far
    second = tap(2) * near
    return jnp.where(row == 0, first, 0.0) + jnp.where(row == 1, second, 0.0)


def whole_mixed(held, prior, taps, slot, feature, columns):
    value = mixed(held, taps, slot, feature, columns)
    return jnp.concatenate([value[0:8] + halo(prior, taps, feature, columns), value[8:]], axis=0)


def handed_on(held, taps, slot, feature, columns):
    tail = held[slot, held.shape[1] - 16 :, columns].astype(jnp.float32)[8:]
    row = lax.broadcasted_iota(jnp.int32, tail.shape, 0)
    tap = lambda lag: taps[lag, feature : feature + 1, columns]
    both = tap(1) * jnp.where(row == 0, pltpu.roll(tail, 1, 0), 0.0)
    return both + tap(2) * jnp.where(row < 2, pltpu.roll(tail, 2, 0), 0.0)


def mix_kernel(features, taps, long_filter, send, tail, token, held, held_last, held_taps, held_filter, edges, sems):
    width = held.shape[2]
    last = held_last.shape[0]
    parts = send.shape[0]
    lanes = width // parts
    quarter = parts * GROUP
    copies = start_all(
        [
            (long_filter, held_filter),
            (taps, held_taps),
            (features.at[1], held.at[0]),
            (features.at[2], held.at[1]),
            (features.at[0, pl.ds(features.shape[1] - last, last)], held_last),
        ],
        sems,
    )
    edges[...] = jnp.zeros_like(edges)
    token[...] = jnp.zeros_like(token)
    copies[0].wait()
    for start in range(0, width, 128):
        store_turned(send, 0, held_filter[:, start : start + 128], start)
    for copy in copies[1:]:
        copy.wait()
    rows = tail.shape[1]
    tail[0] = held_last[last - rows :]
    tail[1:] = held[:, held.shape[1] - rows :]
    row = lax.broadcasted_iota(jnp.int32, (8, 128), 0)
    for start in range(0, width, 128):
        columns = slice(start, start + 128)
        key = mixed(held, held_taps, 0, 1, columns)
        value = mixed(held, held_taps, 1, 2, columns)
        store_turned(send, lanes, key * value, start)
        stack = jnp.where(row < 2, key[0:8], pltpu.roll(value[0:8], 2, 0))
        later = jnp.where(
            row < 2,
            handed_on(held, held_taps, 0, 1, columns),
            pltpu.roll(handed_on(held, held_taps, 1, 2, columns), 2, 0),
        )
        stack = jnp.where(row < 4, stack, pltpu.roll(later, 4, 0))
        top = start // quarter * 8
        edges[top : top + 8, start % quarter : start % quarter + 128] = stack
    for start in range(0, quarter, 128):
        store_turned(send, 2 * lanes, edges[:, start : start + 128], start)


def table_kernel(token, table, out, sems):
    del token
    start_all([(table, out)], sems)[0].wait()


def terms_kernel(token, features, taps, skip, prior, query, direct, held, held_taps, held_skip, sems):
    del token
    width = query.shape[1]
    copies = start_all([(taps, held_taps), (skip, held_skip), (features, held)], sems)
    for copy in copies:
        copy.wait()
    for start in range(0, width, 128):
        columns = slice(start, start + 128)
        part = [whole_mixed(held, prior, held_taps, i, i, columns) for i in range(3)]
        query[:, columns] = part[0].astype(jnp.bfloat16)
        direct[:, columns] = (held_skip[:, columns] * (part[1] * part[2])).astype(jnp.bfloat16)


def rows_of(received, row):
    blocks, _, length = received.shape
    return received[:, row : row + GROUP, :].astype(jnp.float32).reshape(blocks * GROUP, length)


def whole_edges(edge, order):
    length = edge.shape[1]
    nothing = jnp.zeros((GROUP, length), jnp.float32)
    at = lambda block: edge[order.index(block) * GROUP : (order.index(block) + 1) * GROUP]
    before = jnp.concatenate([at(block - 1) if block else nothing for block in order], axis=0)
    joined = edge + pltpu.roll(before, length - 4, 1)
    return joined * pltpu.roll(joined, length - 2, 1)


def patched(signal, edges, index):
    if index:
        edges = pltpu.roll(edges, signal.shape[1] - 8 * index, 1)
    lane = lax.broadcasted_iota(jnp.int32, signal.shape, 1)
    return jnp.where(lane < 2, edges, signal)


def spectrum(groups, ahead, inner_ahead, cosine, sine):
    size, length = groups[0].shape
    both = jnp.dot(ahead, jnp.concatenate(groups, axis=1), preferred_element_type=jnp.float32)
    turned = []
    for i in range(len(groups)):
        real, imag = both[:size, i * length : (i + 1) * length], both[size:, i * length : (i + 1) * length]
        turned.append(jnp.concatenate([real * cosine + imag * sine, imag * cosine - real * sine], axis=1))
    turned = jnp.concatenate(turned, axis=0).astype(jnp.bfloat16)
    return jnp.dot(turned, inner_ahead, preferred_element_type=jnp.float32)


def conv_kernel(order, token, table, received, out):
    del token
    blocks, lanes, length = out.shape
    size = blocks * GROUP
    count = lanes // GROUP
    ahead, (back_real, back_imag), inner_ahead, inner_back, cosine, sine = read_table(table, blocks, length)
    groups = [rows_of(received, i * GROUP).astype(jnp.bfloat16) for i in range(count)]
    other = spectrum(groups, ahead, inner_ahead, cosine, sine)
    edges = whole_edges(rows_of(received, 2 * lanes), order)
    groups = [patched(rows_of(received, lanes + i * GROUP), edges, i).astype(jnp.bfloat16) for i in range(count)]
    part = spectrum(groups, ahead, inner_ahead, cosine, sine)
    xr, xi, hr, hi = part[:, :length], part[:, length:], other[:, :length], other[:, length:]
    joined = jnp.concatenate([xr * hr - xi * hi, xr * hi + xi * hr], axis=1)
    both = jnp.dot(joined.astype(jnp.bfloat16), inner_back, preferred_element_type=jnp.float32)
    reals, imags = [], []
    for i in range(len(groups)):
        real, imag = both[i * size : (i + 1) * size, :length], both[i * size : (i + 1) * size, length:]
        reals.append((real * cosine - imag * sine).astype(jnp.bfloat16))
        imags.append((real * sine + imag * cosine).astype(jnp.bfloat16))
    both = jnp.dot(back_real, jnp.concatenate(reals, axis=1), preferred_element_type=jnp.float32)
    both += jnp.dot(back_imag, jnp.concatenate(imags, axis=1), preferred_element_type=jnp.float32)
    for i in range(count):
        part = both[:, i * length : (i + 1) * length].reshape(blocks, GROUP, length)
        out[:, i * GROUP : (i + 1) * GROUP, :] = part.astype(jnp.bfloat16)


PIECE = 256


def chunk_start(kind, total):
    groups = lax.axis_size("chan")
    step = 1 - 2 * (lax.axis_index("seq") % 2)
    index = (lax.axis_index("chan") + (2, step, groups - step, 0)[kind]) % groups
    return index * (total // groups)


def fetch_columns(weight, first_column, held, sems, first_sem):
    depth, size = held.shape
    copies = []
    for piece in range(depth // PIECE):
        rows = pl.ds(piece * PIECE, PIECE)
        columns = pl.ds(pl.multiple_of(first_column, 128), size)
        copy = pltpu.make_async_copy(weight.at[rows, columns], held.at[rows], sems.at[first_sem + piece])
        copy.start()
        copies.append(copy)
    return copies


def project(gated, held, copies):
    total = None
    for piece, copy in enumerate(copies):
        copy.wait()
        rows = slice(piece * PIECE, (piece + 1) * PIECE)
        part = jnp.dot(gated[:, rows], held[rows, :], preferred_element_type=jnp.float32)
        total = part if total is None else total + part
    return total


def far_kernel(weight, query, direct, conv, gated_out, first_out, second_out, held, sems):
    length, width = query.shape
    quarter = conv.shape[0] * GROUP
    pieces = fetch_columns(weight, chunk_start(0, weight.shape[1]), held, sems, 0)
    for start in range(0, width, 128):
        columns = slice(start, start + 128)
        first = start % quarter // GROUP
        row = start // quarter * GROUP
        turned = conv[first : first + 128 // GROUP, row : row + GROUP, :].astype(jnp.float32)
        turned = turned.reshape(128, length).T
        turned += direct[:, columns].astype(jnp.float32)
        gated_out[:, columns] = (query[:, columns].astype(jnp.float32) * turned).astype(jnp.bfloat16)
    part = project(gated_out, held, pieces).astype(jnp.bfloat16)
    split = second_out.shape[1]
    second_out[...] = part[:, :split]
    first_out[...] = part[:, split:]


def near_kernel(weight, gated, ahead_out, behind_out, ahead_held, behind_held, sems):
    total = weight.shape[1]
    right = ahead_out.shape[1]
    behind_pieces = fetch_columns(weight, chunk_start(2, total) + right, behind_held, sems, 0)
    ahead_pieces = fetch_columns(weight, chunk_start(1, total), ahead_held, sems, len(behind_pieces))
    behind_out[...] = project(gated, behind_held, behind_pieces).astype(jnp.bfloat16)
    ahead_out[...] = project(gated, ahead_held, ahead_pieces).astype(jnp.bfloat16)


def joined_kernel(weight, gated, got, ahead_out, behind_out, ahead_held, behind_held, sems):
    total = weight.shape[1]
    left = behind_out.shape[1]
    behind_pieces = fetch_columns(weight, chunk_start(2, total), behind_held, sems, 0)
    ahead_pieces = fetch_columns(weight, chunk_start(1, total) + left, ahead_held, sems, len(behind_pieces))
    part = project(gated, behind_held, behind_pieces)
    behind_out[...] = (part + got[...].astype(jnp.float32)).astype(jnp.bfloat16)
    ahead_out[...] = project(gated, ahead_held, ahead_pieces).astype(jnp.bfloat16)


def own_kernel(weight, gated, out, held, sems):
    out[...] = project(gated, held, fetch_columns(weight, chunk_start(3, weight.shape[1]), held, sems, 0))


def add_kernel(one, two, out):
    out[...] = (one[...].astype(jnp.float32) + two[...].astype(jnp.float32)).astype(jnp.bfloat16)


def last_kernel(own, first_one, first_two, second_one, second_two, out):
    split = second_one.shape[1]
    wide = lambda ref: ref[...].astype(jnp.float32)
    out[:, :split] = (own[:, :split] + wide(second_one) + wide(second_two)).astype(jnp.bfloat16)
    out[:, split:] = (own[:, split:] + wide(first_one) + wide(first_two)).astype(jnp.bfloat16)


def call(kernel, outs, specs, name, scratch=(), out_specs=None, mebibytes=16):
    return pl.pallas_call(
        kernel,
        out_shape=outs,
        in_specs=specs,
        out_specs=jax.tree.map(lambda _: whole(), outs) if out_specs is None else out_specs,
        scratch_shapes=scratch,
        name=name,
        compiler_params=pltpu.CompilerParams(vmem_limit_bytes=mebibytes * 1024 * 1024),
    )


def shards(features, short_taps, skip_gain, long_filter, out_weight):
    length, width = long_filter.shape
    members = lax.axis_size("seq")
    groups = lax.axis_size("chan")
    lanes = width // members
    size = out_weight.shape[1] // groups
    bf16, f32 = jnp.bfloat16, jnp.float32
    shape = jax.ShapeDtypeStruct
    away = pl.BlockSpec(memory_space=pltpu.HBM)
    loose = pl.BlockSpec(memory_space=pl.ANY)
    inside = whole()
    terms = shape((length, width), bf16)
    turned_shape = shape((members, lanes, length), bf16)
    vmem = lambda dims, dtype: pltpu.VMEM(dims, dtype)
    flags = lambda count: pltpu.SemaphoreType.DMA((count,))

    head = 2 * members // 3
    order = [head] + [i for i in range(members) if i != head]

    def exchange(value):
        return lax.all_to_all(value, "seq", 0, 0, axis_index_groups=[order], tiled=True)

    by_feature = jnp.transpose(features, (1, 0, 2))
    skip = skip_gain[None]
    sending = shape((members, 2 * lanes + GROUP, length), bf16)
    send, tail, token = call(
        mix_kernel,
        (sending, shape((3, 2, width), bf16), shape((8, 128), f32)),
        [away] * 3,
        "mix",
        [
            vmem((2, length, width), bf16),
            vmem((TILE, width), bf16),
            vmem(short_taps.shape, f32),
            vmem((length, width), f32),
            vmem((length, members * GROUP), f32),
            flags(5),
        ],
        mebibytes=60,
    )(by_feature, short_taps, long_filter)
    received = exchange(send)
    prior = lax.ppermute(tail, "seq", [(i, i + 1) for i in range(members - 1)])
    table = transform_table(order, length)
    table = call(table_kernel, shape(table.shape, bf16), [inside, away], "table", [flags(1)])(token, table)
    spectral = call(functools.partial(conv_kernel, order), turned_shape, [loose] + [inside] * 2, "conv")(prior, table, received)
    conv = exchange(spectral)

    def route(sign):
        pairs = []
        for s in range(members):
            for c in range(groups):
                move = sign * (1 - 2 * (s % 2))
                pairs.append((s * groups + c, s * groups + (c + move) % groups))
        return pairs

    def ahead(value):
        return lax.ppermute(value, ("seq", "chan"), route(1))

    def behind(value):
        return lax.ppermute(value, ("seq", "chan"), route(-1))

    split = size // 2
    left, right = shape((length, split), bf16), shape((length, size - split), bf16)
    chunk = vmem((width, size), bf16)
    pieces = width // PIECE
    query, direct = call(
        terms_kernel,
        (terms, terms),
        [loose] + [away] * 3 + [inside],
        "terms",
        [vmem((3, length, width), bf16), vmem(short_taps.shape, f32), vmem(skip.shape, f32), flags(3)],
        mebibytes=50,
    )(spectral, by_feature, short_taps, skip, prior)
    gated, far_first, far_second = call(
        far_kernel,
        (shape((length, width), bf16), right, left),
        [away] + [inside] * 3,
        "far",
        [chunk, flags(pieces)],
        mebibytes=52,
    )(out_weight, query, direct, conv)
    got_first = ahead(far_first)
    got_second = behind(far_second)

    def pair(kernel, ahead_shape, behind_shape, name, *more):
        return call(
            kernel,
            (ahead_shape, behind_shape),
            [away] + [inside] * (1 + len(more)),
            name,
            [vmem((width, ahead_shape.shape[1]), bf16), vmem((width, behind_shape.shape[1]), bf16), flags(2 * pieces)],
            mebibytes=48,
        )(out_weight, gated, *more)

    ahead_out, behind_out = pair(near_kernel, left, right, "near")
    behind_got = behind(behind_out)
    ahead_got = ahead(ahead_out)
    ahead_held, joined = pair(joined_kernel, right, left, "joined", got_second)
    second_got = behind(joined)
    own = call(
        own_kernel, shape((length, size), f32), [away, inside], "own", [chunk, flags(pieces)], mebibytes=48
    )(out_weight, gated)
    first_got = ahead(call(add_kernel, right, [inside] * 2, "add")(got_first, ahead_held))
    return call(last_kernel, shape((length, size), bf16), [inside] * 5, "last")(
        own, first_got, behind_got, ahead_got, second_got
    )


def solution(mesh):
    in_specs = (
        P("seq", None, "chan"),
        P(None, None, "chan"),
        P("chan"),
        P("seq", "chan"),
        P("chan", None),
    )
    out_specs = P("seq", "chan")
    return jax.shard_map(shards, mesh=mesh, in_specs=in_specs, out_specs=out_specs, check_vma=False)
```

```python
import functools
import math

import jax
import jax.numpy as jnp
import ml_dtypes
import numpy as np
from jax import lax
from jax.experimental import pallas as pl
from jax.experimental.pallas import tpu as pltpu
from jax.sharding import PartitionSpec as P

GROUP = 8
TILE = 16


def whole():
    return pl.BlockSpec(memory_space=pltpu.VMEM)


def transform_table(order, length):
    blocks = len(order)
    total = blocks * length
    k1 = np.arange(blocks)[:, None] + 0.25
    outer = 2.0 * math.pi * k1 * np.array(order)[None, :] / blocks
    eye = np.eye(GROUP)
    ahead = np.concatenate([np.kron(np.cos(outer), eye), np.kron(-np.sin(outer), eye)], axis=0)
    back = np.concatenate([np.kron(np.cos(outer).T, eye), np.kron(-np.sin(outer).T, eye)], axis=0) / total
    inner = 2.0 * math.pi * np.outer(np.arange(length), np.arange(length)) / length
    cosine, sine = np.cos(inner), np.sin(inner)
    inner_ahead = np.block([[cosine, -sine], [sine, cosine]])
    inner_back = np.block([[cosine, sine], [-sine, cosine]])
    twist = 2.0 * math.pi * k1 * np.arange(length)[None, :] / total
    twist = np.concatenate([np.cos(twist), np.sin(twist)], axis=1).astype(np.float32)
    high = twist.astype(ml_dtypes.bfloat16)
    low = (twist - high.astype(np.float32)).astype(ml_dtypes.bfloat16)
    parts = [ahead, back, inner_ahead, inner_back, high, low]
    return jnp.asarray(np.concatenate([part.astype(ml_dtypes.bfloat16) for part in parts], axis=0))


def read_table(table, blocks, length):
    size = blocks * GROUP
    at = 4 * size + 4 * length
    twist = table[at : at + blocks, :].astype(jnp.float32) + table[at + blocks : at + 2 * blocks, :].astype(jnp.float32)
    spread = lambda part: jnp.broadcast_to(part[:, None, :], (blocks, GROUP, length)).reshape(size, length)
    return (
        table[: 2 * size, :],
        (table[2 * size : 3 * size, :], table[3 * size : 4 * size, :]),
        table[4 * size : 4 * size + 2 * length, :],
        table[4 * size + 2 * length : at, :],
        spread(twist[:, :length]),
        spread(twist[:, length:]),
    )


def start_all(pairs, sems):
    copies = [pltpu.make_async_copy(source, target, sems.at[i]) for i, (source, target) in enumerate(pairs)]
    for copy in copies:
        copy.start()
    return copies


def store_turned(target, first_row, value, start):
    parts, _, length = target.shape
    first = start % (parts * GROUP) // GROUP
    row = first_row + start // (parts * GROUP) * GROUP
    turned = value.T.reshape(128 // GROUP, GROUP, length).astype(jnp.bfloat16)
    target[first : first + 128 // GROUP, row : row + GROUP, :] = turned


def mixed(features, taps, slot, feature, columns):
    own = features[slot, :, columns].astype(jnp.float32)
    row = lax.broadcasted_iota(jnp.int32, own.shape, 0)
    one = jnp.where(row < 1, 0.0, pltpu.roll(own, 1, 0))
    two = jnp.where(row < 2, 0.0, pltpu.roll(own, 2, 0))
    tap = lambda lag: taps[lag, feature : feature + 1, columns]
    return tap(0) * own + tap(1) * one + tap(2) * two


def halo(prior, taps, feature, columns):
    row = lax.broadcasted_iota(jnp.int32, (8, 128), 0)
    before = prior[feature, :, columns].astype(jnp.float32)
    far, near = before[0:1], before[1:2]
    tap = lambda lag: taps[lag, feature : feature + 1, columns]
    first = tap(1) * near + tap(2) * far
    second = tap(2) * near
    return jnp.where(row == 0, first, 0.0) + jnp.where(row == 1, second, 0.0)


def whole_mixed(held, prior, taps, slot, feature, columns):
    value = mixed(held, taps, slot, feature, columns)
    return jnp.concatenate([value[0:8] + halo(prior, taps, feature, columns), value[8:]], axis=0)


def handed_on(held, taps, slot, feature, columns):
    tail = held[slot, held.shape[1] - 16 :, columns].astype(jnp.float32)[8:]
    row = lax.broadcasted_iota(jnp.int32, tail.shape, 0)
    tap = lambda lag: taps[lag, feature : feature + 1, columns]
    both = tap(1) * jnp.where(row == 0, pltpu.roll(tail, 1, 0), 0.0)
    return both + tap(2) * jnp.where(row < 2, pltpu.roll(tail, 2, 0), 0.0)


def mix_kernel(
    features, taps, long_filter, send_out, tail_out, send, tail, held, held_last, held_taps,
    held_filter, edges, sems
):
    width = held.shape[2]
    last = held_last.shape[0]
    parts = send.shape[0]
    lanes = width // parts
    quarter = parts * GROUP
    copies = start_all(
        [
            (long_filter, held_filter),
            (taps, held_taps),
            (features.at[1], held.at[0]),
            (features.at[2], held.at[1]),
            (features.at[0, pl.ds(features.shape[1] - last, last)], held_last),
        ],
        sems,
    )
    edges[...] = jnp.zeros_like(edges)
    copies[0].wait()
    for start in range(0, width, 128):
        store_turned(send, 0, held_filter[:, start : start + 128], start)
    outs = [pltpu.make_async_copy(send.at[:, pl.ds(0, lanes)], send_out.at[:, pl.ds(0, lanes)], sems.at[5])]
    outs[0].start()
    for copy in copies[1:]:
        copy.wait()
    rows = tail.shape[1]
    tail[0] = held_last[last - rows :]
    tail[1:] = held[:, held.shape[1] - rows :]
    row = lax.broadcasted_iota(jnp.int32, (8, 128), 0)
    for start in range(0, width, 128):
        columns = slice(start, start + 128)
        key = mixed(held, held_taps, 0, 1, columns)
        value = mixed(held, held_taps, 1, 2, columns)
        store_turned(send, lanes, key * value, start)
        stack = jnp.where(row < 2, key[0:8], pltpu.roll(value[0:8], 2, 0))
        later = jnp.where(
            row < 2,
            handed_on(held, held_taps, 0, 1, columns),
            pltpu.roll(handed_on(held, held_taps, 1, 2, columns), 2, 0),
        )
        stack = jnp.where(row < 4, stack, pltpu.roll(later, 4, 0))
        top = start // quarter * 8
        edges[top : top + 8, start % quarter : start % quarter + 128] = stack
    for start in range(0, quarter, 128):
        store_turned(send, 2 * lanes, edges[:, start : start + 128], start)
    rest = pl.ds(lanes, send.shape[1] - lanes)
    outs.append(pltpu.make_async_copy(send.at[:, rest], send_out.at[:, rest], sems.at[6]))
    outs.append(pltpu.make_async_copy(tail, tail_out, sems.at[7]))
    for copy in outs[1:]:
        copy.start()
    for copy in outs:
        copy.wait()


def table_kernel(token, table, out, sems):
    del token
    start_all([(table, out)], sems)[0].wait()


def terms_kernel(token, features, taps, skip, prior, query, direct, held, held_taps, held_skip, sems):
    del token
    width = query.shape[1]
    copies = start_all([(taps, held_taps), (skip, held_skip), (features, held)], sems)
    for copy in copies:
        copy.wait()
    for start in range(0, width, 128):
        columns = slice(start, start + 128)
        part = [whole_mixed(held, prior, held_taps, i, i, columns) for i in range(3)]
        query[:, columns] = part[0].astype(jnp.bfloat16)
        direct[:, columns] = (held_skip[:, columns] * (part[1] * part[2])).astype(jnp.bfloat16)


def rows_of(received, row):
    blocks, _, length = received.shape
    return received[:, row : row + GROUP, :].astype(jnp.float32).reshape(blocks * GROUP, length)


def whole_edges(edge, order):
    length = edge.shape[1]
    nothing = jnp.zeros((GROUP, length), jnp.float32)
    at = lambda block: edge[order.index(block) * GROUP : (order.index(block) + 1) * GROUP]
    before = jnp.concatenate([at(block - 1) if block else nothing for block in order], axis=0)
    joined = edge + pltpu.roll(before, length - 4, 1)
    return joined * pltpu.roll(joined, length - 2, 1)


def patched(signal, edges, index):
    if index:
        edges = pltpu.roll(edges, signal.shape[1] - 8 * index, 1)
    lane = lax.broadcasted_iota(jnp.int32, signal.shape, 1)
    return jnp.where(lane < 2, edges, signal)


def spectrum(groups, ahead, inner_ahead, cosine, sine):
    size, length = groups[0].shape
    both = jnp.dot(ahead, jnp.concatenate(groups, axis=1), preferred_element_type=jnp.float32)
    turned = []
    for i in range(len(groups)):
        real, imag = both[:size, i * length : (i + 1) * length], both[size:, i * length : (i + 1) * length]
        turned.append(jnp.concatenate([real * cosine + imag * sine, imag * cosine - real * sine], axis=1))
    turned = jnp.concatenate(turned, axis=0).astype(jnp.bfloat16)
    return jnp.dot(turned, inner_ahead, preferred_element_type=jnp.float32)


def conv_kernel(order, token, table, received, out):
    del token
    blocks, lanes, length = out.shape
    size = blocks * GROUP
    count = lanes // GROUP
    ahead, (back_real, back_imag), inner_ahead, inner_back, cosine, sine = read_table(table, blocks, length)
    groups = [rows_of(received, i * GROUP).astype(jnp.bfloat16) for i in range(count)]
    other = spectrum(groups, ahead, inner_ahead, cosine, sine)
    edges = whole_edges(rows_of(received, 2 * lanes), order)
    groups = [patched(rows_of(received, lanes + i * GROUP), edges, i).astype(jnp.bfloat16) for i in range(count)]
    part = spectrum(groups, ahead, inner_ahead, cosine, sine)
    xr, xi, hr, hi = part[:, :length], part[:, length:], other[:, :length], other[:, length:]
    joined = jnp.concatenate([xr * hr - xi * hi, xr * hi + xi * hr], axis=1)
    both = jnp.dot(joined.astype(jnp.bfloat16), inner_back, preferred_element_type=jnp.float32)
    reals, imags = [], []
    for i in range(len(groups)):
        real, imag = both[i * size : (i + 1) * size, :length], both[i * size : (i + 1) * size, length:]
        reals.append((real * cosine - imag * sine).astype(jnp.bfloat16))
        imags.append((real * sine + imag * cosine).astype(jnp.bfloat16))
    both = jnp.dot(back_real, jnp.concatenate(reals, axis=1), preferred_element_type=jnp.float32)
    both += jnp.dot(back_imag, jnp.concatenate(imags, axis=1), preferred_element_type=jnp.float32)
    for i in range(count):
        part = both[:, i * length : (i + 1) * length].reshape(blocks, GROUP, length)
        out[:, i * GROUP : (i + 1) * GROUP, :] = part.astype(jnp.bfloat16)


PIECE = 256


def chunk_start(kind, total):
    groups = lax.axis_size("chan")
    step = 1 - 2 * (lax.axis_index("seq") % 2)
    index = (lax.axis_index("chan") + (2, step, groups - step, 0)[kind]) % groups
    return index * (total // groups)


def fetch_columns(weight, first_column, held, sems, first_sem):
    depth, size = held.shape
    copies = []
    for piece in range(depth // PIECE):
        rows = pl.ds(piece * PIECE, PIECE)
        columns = pl.ds(pl.multiple_of(first_column, 128), size)
        copy = pltpu.make_async_copy(weight.at[rows, columns], held.at[rows], sems.at[first_sem + piece])
        copy.start()
        copies.append(copy)
    return copies


def project(gated, held, copies):
    total = None
    for piece, copy in enumerate(copies):
        copy.wait()
        rows = slice(piece * PIECE, (piece + 1) * PIECE)
        part = jnp.dot(gated[:, rows], held[rows, :], preferred_element_type=jnp.float32)
        total = part if total is None else total + part
    return total


def far_kernel(weight, query, direct, conv, gated_out, first_out, second_out, held, sems):
    length, width = query.shape
    quarter = conv.shape[0] * GROUP
    pieces = fetch_columns(weight, chunk_start(0, weight.shape[1]), held, sems, 0)
    for start in range(0, width, 128):
        columns = slice(start, start + 128)
        first = start % quarter // GROUP
        row = start // quarter * GROUP
        turned = conv[first : first + 128 // GROUP, row : row + GROUP, :].astype(jnp.float32)
        turned = turned.reshape(128, length).T
        turned += direct[:, columns].astype(jnp.float32)
        gated_out[:, columns] = (query[:, columns].astype(jnp.float32) * turned).astype(jnp.bfloat16)
    part = project(gated_out, held, pieces).astype(jnp.bfloat16)
    split = second_out.shape[1]
    second_out[...] = part[:, :split]
    first_out[...] = part[:, split:]


def near_kernel(weight, gated, ahead_out, behind_out, ahead_held, behind_held, sems):
    total = weight.shape[1]
    right = ahead_out.shape[1]
    behind_pieces = fetch_columns(weight, chunk_start(2, total) + right, behind_held, sems, 0)
    ahead_pieces = fetch_columns(weight, chunk_start(1, total), ahead_held, sems, len(behind_pieces))
    behind_out[...] = project(gated, behind_held, behind_pieces).astype(jnp.bfloat16)
    ahead_out[...] = project(gated, ahead_held, ahead_pieces).astype(jnp.bfloat16)


def joined_kernel(weight, gated, got, ahead_out, behind_out, ahead_held, behind_held, sems):
    total = weight.shape[1]
    left = behind_out.shape[1]
    behind_pieces = fetch_columns(weight, chunk_start(2, total), behind_held, sems, 0)
    ahead_pieces = fetch_columns(weight, chunk_start(1, total) + left, ahead_held, sems, len(behind_pieces))
    part = project(gated, behind_held, behind_pieces)
    behind_out[...] = (part + got[...].astype(jnp.float32)).astype(jnp.bfloat16)
    ahead_out[...] = project(gated, ahead_held, ahead_pieces).astype(jnp.bfloat16)


def own_kernel(weight, gated, out, held, sems):
    out[...] = project(gated, held, fetch_columns(weight, chunk_start(3, weight.shape[1]), held, sems, 0))


def add_kernel(one, two, out):
    out[...] = (one[...].astype(jnp.float32) + two[...].astype(jnp.float32)).astype(jnp.bfloat16)


def last_kernel(own, first_one, first_two, second_one, second_two, out, held, sems):
    split = second_one.shape[1]
    wide = lambda ref: ref[...].astype(jnp.float32)
    held[:, :split] = (own[:, :split] + wide(second_one) + wide(second_two)).astype(jnp.bfloat16)
    left = pltpu.make_async_copy(held.at[:, pl.ds(0, split)], out.at[:, pl.ds(0, split)], sems.at[0])
    left.start()
    held[:, split:] = (own[:, split:] + wide(first_one) + wide(first_two)).astype(jnp.bfloat16)
    rest = pl.ds(split, out.shape[1] - split)
    right = pltpu.make_async_copy(held.at[:, rest], out.at[:, rest], sems.at[1])
    right.start()
    left.wait()
    right.wait()


def call(kernel, outs, specs, name, scratch=(), out_specs=None, mebibytes=16):
    return pl.pallas_call(
        kernel,
        out_shape=outs,
        in_specs=specs,
        out_specs=jax.tree.map(lambda _: whole(), outs) if out_specs is None else out_specs,
        scratch_shapes=scratch,
        name=name,
        compiler_params=pltpu.CompilerParams(vmem_limit_bytes=mebibytes * 1024 * 1024),
    )


def shards(features, short_taps, skip_gain, long_filter, out_weight):
    length, width = long_filter.shape
    members = lax.axis_size("seq")
    groups = lax.axis_size("chan")
    lanes = width // members
    size = out_weight.shape[1] // groups
    bf16, f32 = jnp.bfloat16, jnp.float32
    shape = jax.ShapeDtypeStruct
    away = pl.BlockSpec(memory_space=pltpu.HBM)
    loose = pl.BlockSpec(memory_space=pl.ANY)
    inside = whole()
    terms = shape((length, width), bf16)
    turned_shape = shape((members, lanes, length), bf16)
    vmem = lambda dims, dtype: pltpu.VMEM(dims, dtype)
    flags = lambda count: pltpu.SemaphoreType.DMA((count,))

    head = 2 * members // 3
    order = [head] + [i for i in range(members) if i != head]

    def exchange(value):
        return lax.all_to_all(value, "seq", 0, 0, axis_index_groups=[order], tiled=True)

    by_feature = jnp.transpose(features, (1, 0, 2))
    skip = skip_gain[None]
    sending = shape((members, 2 * lanes + GROUP, length), bf16)
    send, tail = call(
        mix_kernel,
        (sending, shape((3, 2, width), bf16)),
        [away] * 3,
        "mix",
        [
            vmem(sending.shape, bf16),
            vmem((3, 2, width), bf16),
            vmem((2, length, width), bf16),
            vmem((TILE, width), bf16),
            vmem(short_taps.shape, f32),
            vmem((length, width), f32),
            vmem((length, members * GROUP), f32),
            flags(8),
        ],
        (away,) * 2,
        60,
    )(by_feature, short_taps, long_filter)
    received = exchange(send)
    prior = lax.ppermute(tail, "seq", [(i, i + 1) for i in range(members - 1)])
    table = transform_table(order, length)
    table = call(table_kernel, shape(table.shape, bf16), [loose, away], "table", [flags(1)])(tail, table)
    spectral = call(functools.partial(conv_kernel, order), turned_shape, [loose] + [inside] * 2, "conv")(prior, table, received)
    conv = exchange(spectral)

    def route(sign):
        pairs = []
        for s in range(members):
            for c in range(groups):
                move = sign * (1 - 2 * (s % 2))
                pairs.append((s * groups + c, s * groups + (c + move) % groups))
        return pairs

    def ahead(value):
        return lax.ppermute(value, ("seq", "chan"), route(1))

    def behind(value):
        return lax.ppermute(value, ("seq", "chan"), route(-1))

    split = size // 2
    left, right = shape((length, split), bf16), shape((length, size - split), bf16)
    chunk = vmem((width, size), bf16)
    pieces = width // PIECE
    query, direct = call(
        terms_kernel,
        (terms, terms),
        [loose] + [away] * 3 + [inside],
        "terms",
        [vmem((3, length, width), bf16), vmem(short_taps.shape, f32), vmem(skip.shape, f32), flags(3)],
        mebibytes=50,
    )(spectral, by_feature, short_taps, skip, prior)
    gated, far_first, far_second = call(
        far_kernel,
        (shape((length, width), bf16), right, left),
        [away] + [inside] * 3,
        "far",
        [chunk, flags(pieces)],
        mebibytes=52,
    )(out_weight, query, direct, conv)
    got_first = ahead(far_first)
    got_second = behind(far_second)

    def pair(kernel, ahead_shape, behind_shape, name, *more):
        return call(
            kernel,
            (ahead_shape, behind_shape),
            [away] + [inside] * (1 + len(more)),
            name,
            [vmem((width, ahead_shape.shape[1]), bf16), vmem((width, behind_shape.shape[1]), bf16), flags(2 * pieces)],
            mebibytes=48,
        )(out_weight, gated, *more)

    ahead_out, behind_out = pair(near_kernel, left, right, "near")
    behind_got = behind(behind_out)
    ahead_got = ahead(ahead_out)
    ahead_held, joined = pair(joined_kernel, right, left, "joined", got_second)
    second_got = behind(joined)
    own = call(
        own_kernel, shape((length, size), f32), [away, inside], "own", [chunk, flags(pieces)], mebibytes=48
    )(out_weight, gated)
    first_got = ahead(call(add_kernel, right, [inside] * 2, "add")(got_first, ahead_held))
    out = shape((length, size), bf16)
    return call(last_kernel, out, [inside] * 5, "last", [vmem(out.shape, bf16), flags(2)], away)(
        own, first_got, behind_got, ahead_got, second_got
    )


def solution(mesh):
    in_specs = (
        P("seq", None, "chan"),
        P(None, None, "chan"),
        P("chan"),
        P("seq", "chan"),
        P("chan", None),
    )
    out_specs = P("seq", "chan")
    return jax.shard_map(shards, mesh=mesh, in_specs=in_specs, out_specs=out_specs, check_vma=False)
```

```python
import functools
import math

import jax
import jax.numpy as jnp
import ml_dtypes
import numpy as np
from jax import lax
from jax.experimental import pallas as pl
from jax.experimental.pallas import tpu as pltpu
from jax.sharding import PartitionSpec as P

GROUP = 8
TILE = 16


def whole():
    return pl.BlockSpec(memory_space=pltpu.VMEM)


def transform_table(order, length):
    blocks = len(order)
    total = blocks * length
    k1 = np.arange(blocks)[:, None] + 0.25
    outer = 2.0 * math.pi * k1 * np.array(order)[None, :] / blocks
    eye = np.eye(GROUP)
    ahead = np.concatenate([np.kron(np.cos(outer), eye), np.kron(-np.sin(outer), eye)], axis=0)
    back = np.concatenate([np.kron(np.cos(outer).T, eye), np.kron(-np.sin(outer).T, eye)], axis=0) / total
    inner = 2.0 * math.pi * np.outer(np.arange(length), np.arange(length)) / length
    cosine, sine = np.cos(inner), np.sin(inner)
    inner_ahead = np.block([[cosine, -sine], [sine, cosine]])
    inner_back = np.block([[cosine, sine], [-sine, cosine]])
    twist = 2.0 * math.pi * k1 * np.arange(length)[None, :] / total
    twist = np.concatenate([np.cos(twist), np.sin(twist)], axis=1).astype(np.float32)
    high = twist.astype(ml_dtypes.bfloat16)
    low = (twist - high.astype(np.float32)).astype(ml_dtypes.bfloat16)
    parts = [ahead, back, inner_ahead, inner_back, high, low]
    return jnp.asarray(np.concatenate([part.astype(ml_dtypes.bfloat16) for part in parts], axis=0))


def read_table(table, blocks, length):
    size = blocks * GROUP
    at = 4 * size + 4 * length
    twist = table[at : at + blocks, :].astype(jnp.float32) + table[at + blocks : at + 2 * blocks, :].astype(jnp.float32)
    spread = lambda part: jnp.broadcast_to(part[:, None, :], (blocks, GROUP, length)).reshape(size, length)
    return (
        table[: 2 * size, :],
        (table[2 * size : 3 * size, :], table[3 * size : 4 * size, :]),
        table[4 * size : 4 * size + 2 * length, :],
        table[4 * size + 2 * length : at, :],
        spread(twist[:, :length]),
        spread(twist[:, length:]),
    )


def start_all(pairs, sems):
    copies = [pltpu.make_async_copy(source, target, sems.at[i]) for i, (source, target) in enumerate(pairs)]
    for copy in copies:
        copy.start()
    return copies


def store_turned(target, first_row, value, start):
    parts, _, length = target.shape
    first = start % (parts * GROUP) // GROUP
    row = first_row + start // (parts * GROUP) * GROUP
    turned = value.T.reshape(128 // GROUP, GROUP, length).astype(jnp.bfloat16)
    target[first : first + 128 // GROUP, row : row + GROUP, :] = turned


def mixed(features, taps, slot, feature, columns):
    own = features[slot, :, columns].astype(jnp.float32)
    row = lax.broadcasted_iota(jnp.int32, own.shape, 0)
    one = jnp.where(row < 1, 0.0, pltpu.roll(own, 1, 0))
    two = jnp.where(row < 2, 0.0, pltpu.roll(own, 2, 0))
    tap = lambda lag: taps[lag, feature : feature + 1, columns]
    return tap(0) * own + tap(1) * one + tap(2) * two


def halo(prior, taps, feature, columns):
    row = lax.broadcasted_iota(jnp.int32, (8, 128), 0)
    before = prior[feature, :, columns].astype(jnp.float32)
    far, near = before[0:1], before[1:2]
    tap = lambda lag: taps[lag, feature : feature + 1, columns]
    first = tap(1) * near + tap(2) * far
    second = tap(2) * near
    return jnp.where(row == 0, first, 0.0) + jnp.where(row == 1, second, 0.0)


def whole_mixed(held, prior, taps, slot, feature, columns):
    value = mixed(held, taps, slot, feature, columns)
    return jnp.concatenate([value[0:8] + halo(prior, taps, feature, columns), value[8:]], axis=0)


def handed_on(held, taps, slot, feature, columns):
    tail = held[slot, held.shape[1] - 16 :, columns].astype(jnp.float32)[8:]
    row = lax.broadcasted_iota(jnp.int32, tail.shape, 0)
    tap = lambda lag: taps[lag, feature : feature + 1, columns]
    both = tap(1) * jnp.where(row == 0, pltpu.roll(tail, 1, 0), 0.0)
    return both + tap(2) * jnp.where(row < 2, pltpu.roll(tail, 2, 0), 0.0)


def mix_kernel(
    features, taps, long_filter, send_out, tail_out, send, tail, held, held_last, held_taps,
    held_filter, edges, sems
):
    width = held.shape[2]
    last = held_last.shape[0]
    parts = send.shape[0]
    lanes = width // parts
    quarter = parts * GROUP
    copies = start_all(
        [
            (long_filter, held_filter),
            (taps, held_taps),
            (features.at[1], held.at[0]),
            (features.at[2], held.at[1]),
            (features.at[0, pl.ds(features.shape[1] - last, last)], held_last),
        ],
        sems,
    )
    edges[...] = jnp.zeros_like(edges)
    copies[0].wait()
    for start in range(0, width, 128):
        store_turned(send, 0, held_filter[:, start : start + 128], start)
    outs = [pltpu.make_async_copy(send.at[:, pl.ds(0, lanes)], send_out.at[:, pl.ds(0, lanes)], sems.at[5])]
    outs[0].start()
    for copy in copies[1:]:
        copy.wait()
    rows = tail.shape[1]
    tail[0] = held_last[last - rows :]
    tail[1:] = held[:, held.shape[1] - rows :]
    row = lax.broadcasted_iota(jnp.int32, (8, 128), 0)
    for start in range(0, width, 128):
        columns = slice(start, start + 128)
        key = mixed(held, held_taps, 0, 1, columns)
        value = mixed(held, held_taps, 1, 2, columns)
        store_turned(send, lanes, key * value, start)
        stack = jnp.where(row < 2, key[0:8], pltpu.roll(value[0:8], 2, 0))
        later = jnp.where(
            row < 2,
            handed_on(held, held_taps, 0, 1, columns),
            pltpu.roll(handed_on(held, held_taps, 1, 2, columns), 2, 0),
        )
        stack = jnp.where(row < 4, stack, pltpu.roll(later, 4, 0))
        top = start // quarter * 8
        edges[top : top + 8, start % quarter : start % quarter + 128] = stack
    for start in range(0, quarter, 128):
        store_turned(send, 2 * lanes, edges[:, start : start + 128], start)
    rest = pl.ds(lanes, send.shape[1] - lanes)
    outs.append(pltpu.make_async_copy(send.at[:, rest], send_out.at[:, rest], sems.at[6]))
    outs.append(pltpu.make_async_copy(tail, tail_out, sems.at[7]))
    for copy in outs[1:]:
        copy.start()
    for copy in outs:
        copy.wait()


def table_kernel(token, table, taps, skip, table_out, taps_out, skip_out, sems):
    del token
    for copy in start_all([(table, table_out), (taps, taps_out), (skip, skip_out)], sems):
        copy.wait()


def terms_kernel(token, features, taps, skip, prior, query, direct, held, sems):
    del token
    width = query.shape[1]
    start_all([(features, held)], sems)[0].wait()
    for start in range(0, width, 128):
        columns = slice(start, start + 128)
        part = [whole_mixed(held, prior, taps, i, i, columns) for i in range(3)]
        query[:, columns] = part[0].astype(jnp.bfloat16)
        direct[:, columns] = (skip[:, columns] * (part[1] * part[2])).astype(jnp.bfloat16)


def rows_of(received, row):
    blocks, _, length = received.shape
    return received[:, row : row + GROUP, :].astype(jnp.float32).reshape(blocks * GROUP, length)


def whole_edges(edge, order):
    length = edge.shape[1]
    nothing = jnp.zeros((GROUP, length), jnp.float32)
    at = lambda block: edge[order.index(block) * GROUP : (order.index(block) + 1) * GROUP]
    before = jnp.concatenate([at(block - 1) if block else nothing for block in order], axis=0)
    joined = edge + pltpu.roll(before, length - 4, 1)
    return joined * pltpu.roll(joined, length - 2, 1)


def patched(signal, edges, index):
    if index:
        edges = pltpu.roll(edges, signal.shape[1] - 8 * index, 1)
    lane = lax.broadcasted_iota(jnp.int32, signal.shape, 1)
    return jnp.where(lane < 2, edges, signal)


def spectrum(groups, ahead, inner_ahead, cosine, sine):
    size, length = groups[0].shape
    both = jnp.dot(ahead, jnp.concatenate(groups, axis=1), preferred_element_type=jnp.float32)
    turned = []
    for i in range(len(groups)):
        real, imag = both[:size, i * length : (i + 1) * length], both[size:, i * length : (i + 1) * length]
        turned.append(jnp.concatenate([real * cosine + imag * sine, imag * cosine - real * sine], axis=1))
    turned = jnp.concatenate(turned, axis=0).astype(jnp.bfloat16)
    return jnp.dot(turned, inner_ahead, preferred_element_type=jnp.float32)


def conv_kernel(order, token, table, received, out):
    del token
    blocks, lanes, length = out.shape
    size = blocks * GROUP
    count = lanes // GROUP
    ahead, (back_real, back_imag), inner_ahead, inner_back, cosine, sine = read_table(table, blocks, length)
    groups = [rows_of(received, i * GROUP).astype(jnp.bfloat16) for i in range(count)]
    other = spectrum(groups, ahead, inner_ahead, cosine, sine)
    edges = whole_edges(rows_of(received, 2 * lanes), order)
    groups = [patched(rows_of(received, lanes + i * GROUP), edges, i).astype(jnp.bfloat16) for i in range(count)]
    part = spectrum(groups, ahead, inner_ahead, cosine, sine)
    xr, xi, hr, hi = part[:, :length], part[:, length:], other[:, :length], other[:, length:]
    joined = jnp.concatenate([xr * hr - xi * hi, xr * hi + xi * hr], axis=1)
    both = jnp.dot(joined.astype(jnp.bfloat16), inner_back, preferred_element_type=jnp.float32)
    reals, imags = [], []
    for i in range(len(groups)):
        real, imag = both[i * size : (i + 1) * size, :length], both[i * size : (i + 1) * size, length:]
        reals.append((real * cosine - imag * sine).astype(jnp.bfloat16))
        imags.append((real * sine + imag * cosine).astype(jnp.bfloat16))
    both = jnp.dot(back_real, jnp.concatenate(reals, axis=1), preferred_element_type=jnp.float32)
    both += jnp.dot(back_imag, jnp.concatenate(imags, axis=1), preferred_element_type=jnp.float32)
    for i in range(count):
        part = both[:, i * length : (i + 1) * length].reshape(blocks, GROUP, length)
        out[:, i * GROUP : (i + 1) * GROUP, :] = part.astype(jnp.bfloat16)


PIECE = 256


def chunk_start(kind, total):
    groups = lax.axis_size("chan")
    step = 1 - 2 * (lax.axis_index("seq") % 2)
    index = (lax.axis_index("chan") + (2, step, groups - step, 0)[kind]) % groups
    return index * (total // groups)


def fetch_columns(weight, first_column, held, sems, first_sem):
    depth, size = held.shape
    copies = []
    for piece in range(depth // PIECE):
        rows = pl.ds(piece * PIECE, PIECE)
        columns = pl.ds(pl.multiple_of(first_column, 128), size)
        copy = pltpu.make_async_copy(weight.at[rows, columns], held.at[rows], sems.at[first_sem + piece])
        copy.start()
        copies.append(copy)
    return copies


def project(gated, held, copies):
    total = None
    for piece, copy in enumerate(copies):
        copy.wait()
        rows = slice(piece * PIECE, (piece + 1) * PIECE)
        part = jnp.dot(gated[:, rows], held[rows, :], preferred_element_type=jnp.float32)
        total = part if total is None else total + part
    return total


def far_kernel(weight, query, direct, conv, gated_out, first_out, second_out, held, sems):
    length, width = query.shape
    quarter = conv.shape[0] * GROUP
    pieces = fetch_columns(weight, chunk_start(0, weight.shape[1]), held, sems, 0)
    for start in range(0, width, 128):
        columns = slice(start, start + 128)
        first = start % quarter // GROUP
        row = start // quarter * GROUP
        turned = conv[first : first + 128 // GROUP, row : row + GROUP, :].astype(jnp.float32)
        turned = turned.reshape(128, length).T
        turned += direct[:, columns].astype(jnp.float32)
        gated_out[:, columns] = (query[:, columns].astype(jnp.float32) * turned).astype(jnp.bfloat16)
    part = project(gated_out, held, pieces).astype(jnp.bfloat16)
    split = second_out.shape[1]
    second_out[...] = part[:, :split]
    first_out[...] = part[:, split:]


def near_kernel(weight, gated, ahead_out, behind_out, ahead_held, behind_held, sems):
    total = weight.shape[1]
    right = ahead_out.shape[1]
    behind_pieces = fetch_columns(weight, chunk_start(2, total) + right, behind_held, sems, 0)
    ahead_pieces = fetch_columns(weight, chunk_start(1, total), ahead_held, sems, len(behind_pieces))
    behind_out[...] = project(gated, behind_held, behind_pieces).astype(jnp.bfloat16)
    ahead_out[...] = project(gated, ahead_held, ahead_pieces).astype(jnp.bfloat16)


def joined_kernel(weight, gated, got, ahead_out, behind_out, ahead_held, behind_held, sems):
    total = weight.shape[1]
    left = behind_out.shape[1]
    behind_pieces = fetch_columns(weight, chunk_start(2, total), behind_held, sems, 0)
    ahead_pieces = fetch_columns(weight, chunk_start(1, total) + left, ahead_held, sems, len(behind_pieces))
    part = project(gated, behind_held, behind_pieces)
    behind_out[...] = (part + got[...].astype(jnp.float32)).astype(jnp.bfloat16)
    ahead_out[...] = project(gated, ahead_held, ahead_pieces).astype(jnp.bfloat16)


def own_kernel(weight, gated, out, held, sems):
    out[...] = project(gated, held, fetch_columns(weight, chunk_start(3, weight.shape[1]), held, sems, 0))


def add_kernel(one, two, out):
    out[...] = (one[...].astype(jnp.float32) + two[...].astype(jnp.float32)).astype(jnp.bfloat16)


def last_kernel(own, first_one, first_two, second_one, second_two, out, held, sems):
    split = second_one.shape[1]
    wide = lambda ref: ref[...].astype(jnp.float32)
    held[:, :split] = (own[:, :split] + wide(second_one) + wide(second_two)).astype(jnp.bfloat16)
    left = pltpu.make_async_copy(held.at[:, pl.ds(0, split)], out.at[:, pl.ds(0, split)], sems.at[0])
    left.start()
    held[:, split:] = (own[:, split:] + wide(first_one) + wide(first_two)).astype(jnp.bfloat16)
    rest = pl.ds(split, out.shape[1] - split)
    right = pltpu.make_async_copy(held.at[:, rest], out.at[:, rest], sems.at[1])
    right.start()
    left.wait()
    right.wait()


def call(kernel, outs, specs, name, scratch=(), out_specs=None, mebibytes=16):
    return pl.pallas_call(
        kernel,
        out_shape=outs,
        in_specs=specs,
        out_specs=jax.tree.map(lambda _: whole(), outs) if out_specs is None else out_specs,
        scratch_shapes=scratch,
        name=name,
        compiler_params=pltpu.CompilerParams(vmem_limit_bytes=mebibytes * 1024 * 1024),
    )


def shards(features, short_taps, skip_gain, long_filter, out_weight):
    length, width = long_filter.shape
    members = lax.axis_size("seq")
    groups = lax.axis_size("chan")
    lanes = width // members
    size = out_weight.shape[1] // groups
    bf16, f32 = jnp.bfloat16, jnp.float32
    shape = jax.ShapeDtypeStruct
    away = pl.BlockSpec(memory_space=pltpu.HBM)
    loose = pl.BlockSpec(memory_space=pl.ANY)
    inside = whole()
    terms = shape((length, width), bf16)
    turned_shape = shape((members, lanes, length), bf16)
    vmem = lambda dims, dtype: pltpu.VMEM(dims, dtype)
    flags = lambda count: pltpu.SemaphoreType.DMA((count,))

    head = 2 * members // 3
    order = [head] + [i for i in range(members) if i != head]

    def exchange(value):
        return lax.all_to_all(value, "seq", 0, 0, axis_index_groups=[order], tiled=True)

    by_feature = jnp.transpose(features, (1, 0, 2))
    skip = skip_gain[None]
    sending = shape((members, 2 * lanes + GROUP, length), bf16)
    send, tail = call(
        mix_kernel,
        (sending, shape((3, 2, width), bf16)),
        [away] * 3,
        "mix",
        [
            vmem(sending.shape, bf16),
            vmem((3, 2, width), bf16),
            vmem((2, length, width), bf16),
            vmem((TILE, width), bf16),
            vmem(short_taps.shape, f32),
            vmem((length, width), f32),
            vmem((length, members * GROUP), f32),
            flags(8),
        ],
        (away,) * 2,
        60,
    )(by_feature, short_taps, long_filter)
    received = exchange(send)
    prior = lax.ppermute(tail, "seq", [(i, i + 1) for i in range(members - 1)])
    table = transform_table(order, length)
    table, taps, skip = call(
        table_kernel,
        (shape(table.shape, bf16), shape(short_taps.shape, f32), shape(skip.shape, f32)),
        [loose] + [away] * 3,
        "table",
        [flags(3)],
    )(tail, table, short_taps, skip)
    spectral = call(functools.partial(conv_kernel, order), turned_shape, [loose] + [inside] * 2, "conv")(prior, table, received)
    conv = exchange(spectral)

    def route(sign):
        pairs = []
        for s in range(members):
            for c in range(groups):
                move = sign * (1 - 2 * (s % 2))
                pairs.append((s * groups + c, s * groups + (c + move) % groups))
        return pairs

    def ahead(value):
        return lax.ppermute(value, ("seq", "chan"), route(1))

    def behind(value):
        return lax.ppermute(value, ("seq", "chan"), route(-1))

    split = size // 2
    left, right = shape((length, split), bf16), shape((length, size - split), bf16)
    chunk = vmem((width, size), bf16)
    pieces = width // PIECE
    query, direct = call(
        terms_kernel,
        (terms, terms),
        [loose, away] + [inside] * 3,
        "terms",
        [vmem((3, length, width), bf16), flags(1)],
        mebibytes=50,
    )(spectral, by_feature, taps, skip, prior)
    gated, far_first, far_second = call(
        far_kernel,
        (shape((length, width), bf16), right, left),
        [away] + [inside] * 3,
        "far",
        [chunk, flags(pieces)],
        mebibytes=52,
    )(out_weight, query, direct, conv)
    got_first = ahead(far_first)
    got_second = behind(far_second)

    def pair(kernel, ahead_shape, behind_shape, name, *more):
        return call(
            kernel,
            (ahead_shape, behind_shape),
            [away] + [inside] * (1 + len(more)),
            name,
            [vmem((width, ahead_shape.shape[1]), bf16), vmem((width, behind_shape.shape[1]), bf16), flags(2 * pieces)],
            mebibytes=48,
        )(out_weight, gated, *more)

    ahead_out, behind_out = pair(near_kernel, left, right, "near")
    behind_got = behind(behind_out)
    ahead_got = ahead(ahead_out)
    ahead_held, joined = pair(joined_kernel, right, left, "joined", got_second)
    second_got = behind(joined)
    own = call(
        own_kernel, shape((length, size), f32), [away, inside], "own", [chunk, flags(pieces)], mebibytes=48
    )(out_weight, gated)
    first_got = ahead(call(add_kernel, right, [inside] * 2, "add")(got_first, ahead_held))
    out = shape((length, size), bf16)
    return call(last_kernel, out, [inside] * 5, "last", [vmem(out.shape, bf16), flags(2)], away)(
        own, first_got, behind_got, ahead_got, second_got
    )


def solution(mesh):
    in_specs = (
        P("seq", None, "chan"),
        P(None, None, "chan"),
        P("chan"),
        P("seq", "chan"),
        P("chan", None),
    )
    out_specs = P("seq", "chan")
    return jax.shard_map(shards, mesh=mesh, in_specs=in_specs, out_specs=out_specs, check_vma=False)
```
